256 devices in a mesh: seq: 32 (over z, y), head: 8 (over x, core).
Axes of the slice: x: 4, y: 4, z: 8, core: 2. Of those that a mesh axis runs over, the one named last changes fastest.
Arguments:
- ssm_input: bfloat16 [8192, 8192], P('seq', 'head'), may hold values from -0.59765625 to 0.59765625
- ssm_grad_out: bfloat16 [8192, 8192], P('seq', 'head'), may hold values from -6 to 6
- write_coef: bfloat16 [8192, 128], P('seq'), may hold values from -0.059814453 to 0.059814453
- read_coef: bfloat16 [8192, 128], P('seq'), may hold values from -0.059814453 to 0.059814453
- step_size: float32 [64, 8192], P('head', 'seq'), may hold values from 0.25 to 4
- decay_rate: float32 [64], P('head'), may hold values from 5e-05 to 0.1
- skip_gain: float32 [64], P('head'), may hold values from 0.5 to 1.5
- queries: bfloat16 [8192, 4096], P('seq', 'head'), may hold values from -8 to 8
- att_keys: bfloat16 [8192, 1024], P('seq', 'head'), may hold values from -8 to 8
- att_values: bfloat16 [8192, 1024], P('seq', 'head'), may hold values from -6 to 6
- out_grad: bfloat16 [8192, 4096], P('seq', 'head'), may hold values from -6 to 6
- doc_lengths: int32 [128], replicated, may hold values from 1 to 1024, 8192 in all
Outputs:
- grad_input: bfloat16 [8192, 8192], P('seq', 'head')
- grad_write: float32 [8192, 128], P(('seq', 'head'))
- grad_read: float32 [8192, 128], P(('seq', 'head'))
- grad_query: bfloat16 [8192, 4096], P('seq', 'head')
- grad_key: bfloat16 [8192, 1024], P('seq', 'head')
- grad_value: bfloat16 [8192, 1024], P('seq', 'head')
The draws below stay inside these ranges and needn't reach their ends.
Inputs may be any that keep to these rules, and one draw needn't show every extreme that they name: `doc_lengths`: they sum to 8192; the longest document has exactly 1024 tokens.
All inputs are finite; a program needn't handle non-finite values.
Results may differ from the reference program's by a relative error of at most 0.0085.
Values may be sent and summed in bfloat16 or wider, within the bound.
A program may use at most 128 MiB of HBM per device.

```python
import math
import jax
import jax.numpy as jnp
import numpy as np
from jax import lax

TOK_DEV = 256
SSM_HEADS = 64
SSM_DIM = 128
STATE = 128
Q_HEADS = 32
KV_HEADS = 8
HEAD_DIM = 128
REACH = 4
ALL_SEQ_ITEMS = 8192
DOCS = 128
DOC_MOST = 1024
N_SEQ = 32


def attention_pair(key):
    foundation_prng_seed = jax.random.fold_in(key, 7103)
    key_query, key_keys = jax.random.split(foundation_prng_seed, 2)
    query_vals = jnp.clip(jax.random.normal(key_query, (ALL_SEQ_ITEMS, Q_HEADS * HEAD_DIM), jnp.float32), -6.0, 6.0)
    key_vals = jnp.clip(jax.random.normal(key_keys, (ALL_SEQ_ITEMS, KV_HEADS * HEAD_DIM), jnp.float32), -6.0, 6.0)
    return (query_vals, key_vals)


def draw_queries(key, part):
    return attention_pair(key)[0].astype(jnp.bfloat16)


def draw_att_keys(key, part):
    return attention_pair(key)[1].astype(jnp.bfloat16)


def draw_step_size(key, part):
    foundation_prng_seed = jax.random.fold_in(key, 2207)
    root_sampler_seed, lookup_tile_lines = jax.random.split(foundation_prng_seed, 2)
    steady = jnp.exp(jax.random.uniform(root_sampler_seed, (SSM_HEADS, ALL_SEQ_ITEMS), jnp.float32, math.log(0.5), math.log(2.0)))
    block_scale = jnp.exp(jax.random.uniform(lookup_tile_lines, (ALL_SEQ_ITEMS // TOK_DEV,), jnp.float32, math.log(0.5), math.log(2.0)))
    return (steady * jnp.repeat(block_scale, TOK_DEV)[None, :]).astype(jnp.float32)


def draw_decay_rate(key, part):
    foundation_prng_seed = jax.random.fold_in(key, 3301)
    key_kind, key_fast, key_slow = jax.random.split(foundation_prng_seed, 3)
    fast_share = 0.5
    is_fast = jax.random.bernoulli(key_kind, fast_share, (SSM_HEADS,))
    fast_level = jnp.exp(jax.random.uniform(key_fast, (SSM_HEADS,), jnp.float32, math.log(0.7), math.log(1.6)))
    slow_level = jnp.exp(jax.random.uniform(key_slow, (SSM_HEADS,), jnp.float32, math.log(0.06), math.log(0.4)))
    block_level = jnp.where(is_fast, fast_level, slow_level)
    return (block_level / TOK_DEV).astype(jnp.float32)


def shard_levels(key, shape, cuts, least, top_value):
    def one(position, blocks):
        draws = jax.random.uniform(jax.random.fold_in(jax.random.fold_in(key, 6), position), (blocks,), jnp.float32, least / len(cuts), top_value / len(cuts))
        return jnp.repeat(jnp.exp(draws), shape[position] // blocks).reshape((-1,) + (1,) * (len(shape) - position - 1))

    factor_of = one(*cuts[0])
    for cut in cuts[1:]:
        factor_of = factor_of * one(*cut)
    return factor_of


def profile(amount, total, most, slope):
    portions = [(1 << 20) // math.isqrt(standing ** slope) + 1 for standing in range(2, amount + 1)]
    spare, counts = total - most - (amount - 1), [1] * (amount - 1)
    while spare > 0:
        movable = [i for i in range(amount - 1) if counts[i] < most]
        pool, remaining = sum([portions[i] for i in movable]), spare
        for i in movable:
            more = min(most - counts[i], max(1, remaining * portions[i] // pool), spare)
            counts[i] = counts[i] + more
            spare = spare - more
    return np.array([most] + counts)


def ragged_sizes(stream_key, amount, total, most, lean):
    if amount == 2:
        one = jax.random.randint(stream_key, (), max(1, total - most), min(most, total - 1) + 1)
        return jnp.stack([one, total - one])
    lengths = jnp.asarray(profile(amount, total, most, lean), jnp.int32)
    pairs = (amount - 1) // 2
    giver, taker = lengths[1:1 + 2 * pairs:2], lengths[2:2 + 2 * pairs:2]
    room = jnp.minimum(giver - 1, most - taker)
    passed = jax.random.randint(jax.random.fold_in(stream_key, 1), (pairs,), 0, 1 << 20) % (room + 1)
    lengths = lengths.at[1:1 + 2 * pairs:2].set(giver - passed).at[2:2 + 2 * pairs:2].set(taker + passed)
    return lengths[jax.random.permutation(jax.random.fold_in(stream_key, 2), amount)]


def bell_draw(key, extent, width, limit, shards=(), held_as=jnp.bfloat16):
    factor_of = shard_levels(key, extent, shards, -0.22, 0.18) if shards else 1.0
    values = jax.random.normal(key, extent, jnp.float32) * width * factor_of
    return jnp.minimum(jnp.maximum(values, -limit), limit).astype(held_as)


def setup_inputs(seed: int = 0) -> dict:
    key_of = jax.random.split(jax.random.key(seed), 13)
    return {
        "ssm_input": bell_draw(key_of[0], (ALL_SEQ_ITEMS, SSM_HEADS * SSM_DIM), 0.1, 0.59765625, ((0, 32), (1, 8))),
        "ssm_grad_out": bell_draw(key_of[1], (ALL_SEQ_ITEMS, SSM_HEADS * SSM_DIM), 1.0, 6.0, ((0, 32), (1, 8))),
        "write_coef": bell_draw(key_of[2], (ALL_SEQ_ITEMS, STATE), 0.01, 0.059814453, ((0, 32),)),
        "read_coef": bell_draw(key_of[3], (ALL_SEQ_ITEMS, STATE), 0.01, 0.059814453, ((0, 32),)),
        "step_size": draw_step_size(jax.random.fold_in(key_of[12], 71), 0),
        "decay_rate": draw_decay_rate(jax.random.fold_in(key_of[12], 71), 0),
        "skip_gain": jnp.clip(1.0 + 0.1 * jax.random.normal(key_of[6], (SSM_HEADS,), jnp.float32), 0.5, 1.5),
        "queries": draw_queries(jax.random.fold_in(key_of[12], 71), 0),
        "att_keys": draw_att_keys(jax.random.fold_in(key_of[12], 71), 0),
        "att_values": bell_draw(key_of[9], (ALL_SEQ_ITEMS, KV_HEADS * HEAD_DIM), 1.0, 6.0, ((0, 32), (1, 8))),
        "out_grad": bell_draw(key_of[10], (ALL_SEQ_ITEMS, Q_HEADS * HEAD_DIM), 1.0, 6.0, ((0, 32), (1, 8))),
        "doc_lengths": ragged_sizes(key_of[11], DOCS, ALL_SEQ_ITEMS, DOC_MOST, 2).astype(jnp.int32),
    }


neg_fill = -1e30


def half_round(values):
    return lax.optimization_barrier(values.astype(jnp.bfloat16)).astype(jnp.float32)


def doc_starts(doc_lengths, element_indices):
    doc_ends = jnp.cumsum(doc_lengths, dtype=jnp.int32)
    doc_first = doc_ends - doc_lengths
    chosen = jnp.where(doc_first[None, :] <= element_indices[:, None], doc_first[None, :], jnp.zeros_like(doc_first)[None, :])
    return jnp.max(chosen, axis=1)


def reset_factors(running, first_blk, block_first):
    totals = running[:, -1]
    began_before = first_blk < block_first
    continues = first_blk == first_blk[-1]
    tail_decay = jnp.where(continues[None, :], jnp.exp(totals[:, None] - running), 0.0)
    lead_decay = jnp.where(began_before[None, :], jnp.exp(running), 0.0)
    decay_total = jnp.where(began_before[-1], jnp.exp(totals), jnp.zeros_like(totals))
    return tail_decay, lead_decay, decay_total


def ssd_summary(inputs_blk, grads_blk, write_blk, read_blk, step_blk, first_blk, block_first, decay_rate):
    length = inputs_blk.shape[0]
    heads_here = decay_rate.shape[0]
    running = jnp.cumsum(-decay_rate[:, None] * step_blk, axis=1)
    tail_decay, lead_decay, decay_total = reset_factors(running, first_blk, block_first)
    inputs3 = inputs_blk.reshape(length, heads_here, -1).astype(jnp.float32)
    grads3 = grads_blk.reshape(length, heads_here, -1).astype(jnp.float32)
    write_scaled = half_round(tail_decay[:, :, None] * write_blk.astype(jnp.float32)[None])
    read_scaled = half_round(lead_decay[:, :, None] * read_blk.astype(jnp.float32)[None])
    state_part = jnp.einsum("hsn,shp->hnp", write_scaled, inputs3)
    adjoint_part = jnp.einsum("htn,thp->hnp", read_scaled, grads3)
    return decay_total, state_part, adjoint_part


def ssd_block_grads(inputs_blk, grads_blk, write_blk, read_blk, step_blk, first_blk, block_first, decay_rate, skip_gain, state_in, adjoint_in):
    length = inputs_blk.shape[0]
    heads_here = decay_rate.shape[0]
    running = jnp.cumsum(-decay_rate[:, None] * step_blk, axis=1)
    tail_decay, lead_decay, _ = reset_factors(running, first_blk, block_first)
    lower_tri = (jnp.arange(length)[:, None] >= jnp.arange(length)[None, :]) & (first_blk[:, None] == first_blk[None, :])
    spread = running[:, :, None] - running[:, None, :]
    decay_mat = jnp.where(lower_tri[None], jnp.exp(jnp.where(lower_tri[None], spread, 0.0)), 0.0)
    inputs3 = inputs_blk.reshape(length, heads_here, -1).astype(jnp.float32)
    grads3 = grads_blk.reshape(length, heads_here, -1).astype(jnp.float32)
    write_full = write_blk.astype(jnp.float32)
    read_full = read_blk.astype(jnp.float32)
    corr_mat = jnp.einsum("thp,shp->hts", grads3, inputs3)
    weight_mat = half_round(corr_mat * decay_mat)
    cross_mat = jnp.dot(read_blk, write_blk.T, preferred_element_type=jnp.float32)
    mix_mat = half_round(cross_mat[None] * decay_mat)
    state_half = half_round(state_in)
    adjoint_half = half_round(adjoint_in)
    input_local = jnp.einsum("hst,shp->thp", mix_mat, grads3)
    input_carry = jnp.einsum("tn,hnp->thp", write_full, adjoint_half) * tail_decay.T[:, :, None]
    grad_input = (skip_gain[None, :, None] * grads3 + input_local + input_carry).astype(jnp.bfloat16)
    write_local = jnp.einsum("hst,sn->tn", weight_mat, read_full)
    write_carry = jnp.einsum("thp,hnp->htn", inputs3, adjoint_half)
    grad_write = write_local + jnp.sum(tail_decay[:, :, None] * write_carry, axis=0)
    read_local = jnp.einsum("hts,sn->tn", weight_mat, write_full)
    read_carry = jnp.einsum("thp,hnp->htn", grads3, state_half)
    grad_read = read_local + jnp.sum(lead_decay[:, :, None] * read_carry, axis=0)
    return grad_input.reshape(length, -1), grad_write, grad_read


def attention_grads(queries, att_keys, att_values, out_grad, doc_lengths):
    window = (REACH + 1) * TOK_DEV
    scale_factor = HEAD_DIM ** -0.5
    group_size = Q_HEADS // KV_HEADS
    front_pad = jnp.zeros((REACH * TOK_DEV, KV_HEADS * HEAD_DIM), jnp.bfloat16)
    pad_keys = jnp.concatenate([front_pad, att_keys], axis=0)
    pad_values = jnp.concatenate([front_pad, att_values], axis=0)

    def one_block(carried, block_index):
        first = (block_index * TOK_DEV).astype(jnp.int32)
        query_blk = lax.dynamic_slice_in_dim(queries, first, TOK_DEV, 0).reshape(TOK_DEV, KV_HEADS, group_size, HEAD_DIM).astype(jnp.float32)
        grad_blk = lax.dynamic_slice_in_dim(out_grad, first, TOK_DEV, 0).reshape(TOK_DEV, KV_HEADS, group_size, HEAD_DIM).astype(jnp.float32)
        key_win = lax.dynamic_slice_in_dim(pad_keys, first, window, 0).reshape(window, KV_HEADS, HEAD_DIM).astype(jnp.float32)
        value_win = lax.dynamic_slice_in_dim(pad_values, first, window, 0).reshape(window, KV_HEADS, HEAD_DIM).astype(jnp.float32)
        query_pos = first + jnp.arange(TOK_DEV, dtype=jnp.int32)
        key_pos = first - REACH * TOK_DEV + jnp.arange(window, dtype=jnp.int32)
        first_pos = doc_starts(doc_lengths, query_pos)
        key_mask = (key_pos[None, :] >= first_pos[:, None]) & (key_pos[None, :] <= query_pos[:, None])
        scores = jnp.einsum("tkgd,skd->kgts", query_blk, key_win) * scale_factor
        scores = jnp.where(key_mask[None, None], scores, neg_fill)
        row_max = jnp.max(scores, axis=-1, keepdims=True)
        weights = jnp.where(key_mask[None, None], jnp.exp(scores - row_max), 0.0)
        probs = weights / jnp.sum(weights, axis=-1, keepdims=True)
        probs_half = half_round(probs)
        attended = jnp.einsum("kgts,skd->tkgd", probs_half, value_win)
        delta_rows = jnp.sum(grad_blk * attended, axis=-1)
        dprob = jnp.einsum("tkgd,skd->kgts", grad_blk, value_win)
        dscore = half_round(probs * (dprob - jnp.transpose(delta_rows, (1, 2, 0))[..., None]))
        grad_q = (jnp.einsum("kgts,skd->tkgd", dscore, key_win) * scale_factor).astype(jnp.bfloat16)
        grad_k = jnp.einsum("kgts,tkgd->skd", dscore, query_blk) * scale_factor
        grad_v = jnp.einsum("kgts,tkgd->skd", probs_half, grad_blk)
        both_parts = jnp.stack((grad_k, grad_v)).reshape(2, window, KV_HEADS * HEAD_DIM)
        current = lax.dynamic_slice_in_dim(carried, first, window, 1)
        carried = lax.dynamic_update_slice_in_dim(carried, current + both_parts, first, 1)
        return carried, grad_q.reshape(TOK_DEV, Q_HEADS * HEAD_DIM)

    start_acc = jnp.zeros((2, (N_SEQ + REACH) * TOK_DEV, KV_HEADS * HEAD_DIM), jnp.float32)
    final_acc, grad_query = lax.scan(one_block, start_acc, jnp.arange(N_SEQ, dtype=jnp.int32))
    grad_pair = final_acc[:, REACH * TOK_DEV:].astype(jnp.bfloat16)
    return grad_query.reshape(ALL_SEQ_ITEMS, Q_HEADS * HEAD_DIM), grad_pair[0], grad_pair[1]


def reference(ssm_input, ssm_grad_out, write_coef, read_coef, step_size, decay_rate, skip_gain, queries, att_keys, att_values, out_grad, doc_lengths):
    blocks_in = ssm_input.reshape(N_SEQ, TOK_DEV, -1)
    blocks_grad = ssm_grad_out.reshape(N_SEQ, TOK_DEV, -1)
    blocks_write = write_coef.reshape(N_SEQ, TOK_DEV, -1)
    blocks_read = read_coef.reshape(N_SEQ, TOK_DEV, -1)
    blocks_step = step_size.reshape(SSM_HEADS, N_SEQ, TOK_DEV).transpose(1, 0, 2)
    all_first = doc_starts(doc_lengths, jnp.arange(ALL_SEQ_ITEMS, dtype=jnp.int32))
    blocks_first = all_first.reshape(N_SEQ, TOK_DEV)
    block_starts = (jnp.arange(N_SEQ, dtype=jnp.int32) * TOK_DEV).astype(jnp.int32)
    decays, states, adjoints = lax.map(
        lambda items: ssd_summary(items[0], items[1], items[2], items[3], items[4], items[5], items[6], decay_rate),
        (blocks_in, blocks_grad, blocks_write, blocks_read, blocks_step, blocks_first, block_starts))

    def forward_step(carried, items):
        return items[0][:, None, None] * carried + items[1], carried

    def backward_step(carried, items):
        return items[1] + items[0][:, None, None] * carried, carried

    zero_state = jnp.zeros((SSM_HEADS, STATE, SSM_DIM), jnp.float32)
    _, state_in = lax.scan(forward_step, zero_state, (decays, states))
    _, adjoint_in = lax.scan(backward_step, zero_state, (decays, adjoints), reverse=True)
    grad_input, grad_write, grad_read = lax.map(
        lambda items: ssd_block_grads(items[0], items[1], items[2], items[3], items[4], items[5], items[6], decay_rate, skip_gain, items[7], items[8]),
        (blocks_in, blocks_grad, blocks_write, blocks_read, blocks_step, blocks_first, block_starts, state_in, adjoint_in))
    grad_query, grad_key, grad_value = attention_grads(queries, att_keys, att_values, out_grad, doc_lengths)
    return (grad_input.reshape(ALL_SEQ_ITEMS, -1), grad_write.reshape(ALL_SEQ_ITEMS, STATE), grad_read.reshape(ALL_SEQ_ITEMS, STATE),
            grad_query, grad_key, grad_value)
```

```python
import functools
import math

import jax
import jax.numpy as jnp
from jax import lax
from jax.experimental import pallas as pl
from jax.experimental.pallas import tpu as pltpu
from jax.sharding import PartitionSpec as P

MESH = pl.DeviceIdType.MESH
REACH = 4
DIM = 128
NEG = -1e30
SCALE = DIM ** (-0.5)
SCALE2 = SCALE * math.log2(math.e)
SHIFT = 1

F32 = jnp.float32
BF16 = jnp.bfloat16


def nn(a, b):
    return jnp.dot(a, b, preferred_element_type=F32)


def nt(a, b):
    return lax.dot_general(a, b, (((1,), (1,)), ((), ())), preferred_element_type=F32)


def flip(a):
    return jnp.transpose(a.astype(F32))


def cols(h):
    return pl.ds(pl.multiple_of(h * DIM, DIM), DIM)


def kernel(
    n_seq,
    n_head,
    x_ref,
    g_ref,
    w_ref,
    r_ref,
    step_ref,
    rate_ref,
    gain_ref,
    q_ref,
    k_ref,
    v_ref,
    og_ref,
    doc_ref,
    gi_ref,
    gw_ref,
    gr_ref,
    gq_ref,
    gk_ref,
    gv_ref,
    kv,
    kt,
    dacc,
    dkv_out,
    dkv_in,
    cbuf,
    st_out,
    st_in,
    wt,
    rt,
    rows,
    run_col,
    tail_col,
    lead_col,
    gi_acc,
    w_acc,
    coef,
    tot,
    rs_in,
    kv_send,
    kv_recv,
    c_send,
    c_recv,
    st_send,
    st_recv,
    dkv_send,
    dkv_recv,
    rs_send,
    rs_recv,
):
    tok = x_ref.shape[0]
    heads = step_ref.shape[0]
    q_heads = q_ref.shape[1] // DIM
    me = lax.axis_index("seq")
    hd = lax.axis_index("head")

    def seq_at(d):
        return lax.rem(me + (d + n_seq), n_seq)

    def head_at(p):
        return lax.rem(hd + p, n_head)

    def push(src, dst, send, recv, to):
        return pltpu.make_async_remote_copy(
            src_ref=src, dst_ref=dst, send_sem=send, recv_sem=recv, device_id=to, device_id_type=MESH
        )

    barrier = pltpu.get_barrier_semaphore()
    offsets = [d for d in range(-REACH, REACH + 1) if d]
    for d in offsets:
        pl.semaphore_signal(barrier, inc=1, device_id=(seq_at(d), hd), device_id_type=MESH)
    for p in range(1, n_head):
        pl.semaphore_signal(barrier, inc=1, device_id=(me, head_at(p)), device_id_type=MESH)

    kv[0, 0] = k_ref[...]
    kv[0, 1] = v_ref[...]

    pl.semaphore_wait(barrier, len(offsets) + n_head - 1)

    kv_copies = {}
    for d in (4, 1, 3, 2):
        kv_copies[d] = push(
            kv.at[0], kv.at[d], kv_send.at[d - 1], kv_recv.at[d - 1], (seq_at(d), hd)
        )
        kv_copies[d].start()

    base = (me * tok).astype(F32)
    lens = jnp.broadcast_to(doc_ref[...].astype(F32), (DIM, DIM))
    i0 = lax.broadcasted_iota(jnp.int32, (DIM, DIM), 0)
    i1 = lax.broadcasted_iota(jnp.int32, (DIM, DIM), 1)
    first_c = jnp.sum(jnp.where(i1 < i0, lens, 0.0), axis=1, keepdims=True)
    lens_c = jnp.sum(jnp.where(i1 == i0, lens, 0.0), axis=1, keepdims=True)
    first_r = jnp.sum(jnp.where(i0 < i1, lens_c, 0.0), axis=0, keepdims=True)
    t_row = base + lax.broadcasted_iota(jnp.int32, (1, tok), 1).astype(F32)
    t_col = base + lax.broadcasted_iota(jnp.int32, (tok, 1), 0).astype(F32)
    fp_row = jnp.max(jnp.where(first_c <= t_row, first_c, 0.0), axis=0, keepdims=True)
    fp_col = jnp.max(jnp.where(first_r <= t_col, first_r, 0.0), axis=1, keepdims=True)
    fp_last = fp_row[:, tok - 1 : tok]

    sub = lax.broadcasted_iota(jnp.int32, (heads, 1), 0)
    rate = jnp.zeros((heads, 1), F32)
    for h in range(heads):
        rate = jnp.where(sub == h, rate_ref[h], rate)
    decay = -(rate * step_ref[...])
    j0 = lax.broadcasted_iota(jnp.int32, (tok, tok), 0)
    j1 = lax.broadcasted_iota(jnp.int32, (tok, tok), 1)
    run_r = jnp.dot(
        decay,
        (j0 <= j1).astype(F32),
        preferred_element_type=F32,
        precision=lax.Precision.HIGHEST,
    )
    run_c = lax.dot_general(
        (j1 <= j0).astype(F32),
        decay,
        (((1,), (1,)), ((), ())),
        preferred_element_type=F32,
        precision=lax.Precision.HIGHEST,
    )
    total_c = run_r[:, tok - 1 : tok]
    total_r = run_c[tok - 1 : tok, :]
    rows[0] = run_r
    rows[1] = jnp.where(fp_row == fp_last, jnp.exp(total_c - run_r), 0.0)
    rows[2] = jnp.where(fp_row < base, jnp.exp(run_r), 0.0)
    cbuf[3] = jnp.broadcast_to(jnp.where(fp_last < base, jnp.exp(total_c), 0.0), (heads, DIM))
    c_copies = []
    for i, d in enumerate((-3, -2, -1, 1, 2, 3)):
        copy = push(cbuf.at[3], cbuf.at[3 - d], c_send.at[i], c_recv.at[3 - d], (seq_at(d), hd))
        copy.start()
        c_copies.append(copy)

    wt[...] = flip(w_ref[...])
    rt[...] = flip(r_ref[...])

    def part_loop(h, _):
        scaled_w = (wt[...] * rows[1, pl.ds(h, 1), :]).astype(BF16)
        scaled_r = (rt[...] * rows[2, pl.ds(h, 1), :]).astype(BF16)
        st_out[0, 0, h] = nn(scaled_w, x_ref[:, cols(h)]).astype(BF16)
        st_out[1, 0, h] = nn(scaled_r, g_ref[:, cols(h)]).astype(BF16)
        return 0

    lax.fori_loop(0, heads, part_loop, 0)

    pos = (lax.rem(me, 4), lax.rem(3 + SHIFT + n_seq - me, 4))
    sign = (1, -1)
    st_copies = {}

    def send_state(which, stage):
        y = pos[which]
        if stage == 0:
            step = 1 - 2 * lax.rem(y, 2)
        elif stage == 1:
            step = 3 - 2 * y
        else:
            step = 4
        to = lax.rem(me + sign[which] * step + n_seq, n_seq)
        copy = push(
            st_out.at[which, stage],
            st_in.at[which, stage],
            st_send.at[which, stage],
            st_recv.at[which, stage],
            (to, hd),
        )
        copy.start()
        st_copies[which, stage] = copy

    send_state(0, 0)
    send_state(1, 0)

    tail_c = jnp.where(fp_col == fp_last, jnp.exp(total_r - run_c), 0.0)
    lead_c = jnp.where(fp_col < base, jnp.exp(run_c), 0.0)
    for h in range(heads):
        run_col[h] = run_c[:, h : h + 1]
        tail_col[h] = tail_c[:, h : h + 1]
        lead_col[h] = lead_c[:, h : h + 1]

    cross = nt(w_ref[...], r_ref[...])
    keep = (j0 <= j1) & (fp_col == fp_row)
    w_acc[...] = jnp.zeros_like(w_acc)

    def local_loop(h, _):
        x_h = x_ref[:, cols(h)]
        g_h = g_ref[:, cols(h)]
        corr = nt(x_h, g_h)
        dec = jnp.exp(jnp.where(keep, rows[0, pl.ds(h, 1), :] - run_col[h], NEG))
        w_acc[...] += corr * dec
        mix = (cross * dec).astype(BF16)
        gi_acc[:, cols(h)] = nn(mix, g_h) + gain_ref[h] * g_h.astype(F32)
        return 0

    lax.fori_loop(0, heads, local_loop, 0)
    w_sum = w_acc[...]
    gw = nn(w_sum.astype(BF16), r_ref[...])
    gr = nn(flip(w_sum).astype(BF16), w_ref[...])
    for c in range(n_head):
        tot[c, 0] = gw[c * (tok // n_head) : (c + 1) * (tok // n_head)]
        tot[c, 1] = gr[c * (tok // n_head) : (c + 1) * (tok // n_head)]

    for copy in c_copies:
        copy.wait_recv()
    for which in (0, 1):
        y, s = pos[which], sign[which]
        c0, c1, c2, c3 = [cbuf[3 + s * (q - y)] for q in range(4)]
        own, after = cbuf[3], cbuf[3 + s]
        odd = lax.rem(y, 2) == 1
        one, zero = jnp.ones_like(own), jnp.zeros_like(own)
        coef[which, 0] = jnp.where(odd, one, after)
        coef[which, 1] = jnp.where(odd, own, one)
        coef[which, 2] = jnp.where(y < 2, c2 * c3, one)
        coef[which, 3] = jnp.where(y < 2, one, zero)
        coef[which, 4] = jnp.where(odd, one, zero)
        coef[which, 5] = jnp.where(y == 2, one, jnp.where(y == 3, c2, zero))
        coef[which, 6] = jnp.where(
            y == 0, one, jnp.where(y == 1, c0, jnp.where(y == 2, c0 * c1, c0 * c1 * c2))
        )

    def factor(which, i, h):
        return coef[which, i, pl.ds(h, 1), :]

    for which in (0, 1):
        st_copies[which, 0].wait_recv()

        def pair_loop(h, _, which=which):
            st_out[which, 1, h] = (
                factor(which, 0, h) * st_out[which, 0, h].astype(F32)
                + factor(which, 1, h) * st_in[which, 0, h].astype(F32)
            ).astype(BF16)
            return 0

        lax.fori_loop(0, heads, pair_loop, 0)
        send_state(which, 1)

    for d in (4, 1, 3, 2):
        kv_copies[d].wait_recv()
    for o in range(REACH + 1):
        kt[o] = flip(kv[o, 0]).astype(BF16)
    dacc[...] = jnp.zeros_like(dacc)
    spot = lax.broadcasted_iota(jnp.int32, (tok, 1), 0).astype(F32)

    def attend(i, _):
        q_i = q_ref[:, cols(i)]
        og_i = og_ref[:, cols(i)]
        scores = []
        for o in range(REACH + 1):
            key_pos = spot + (base - float(o * tok))
            allowed = key_pos >= fp_row
            if o == 0:
                allowed = allowed & (key_pos <= t_row)
            scores.append(jnp.where(allowed, nt(kv[o, 0], q_i) * SCALE2, NEG))
        top = functools.reduce(jnp.maximum, [jnp.max(s, axis=0, keepdims=True) for s in scores])
        weights = [jnp.exp2(s - top) for s in scores]
        norm = 1.0 / functools.reduce(
            jnp.add, [jnp.sum(e, axis=0, keepdims=True) for e in weights]
        )
        probs = [e * norm for e in weights]
        halves = [p.astype(BF16) for p in probs]
        dprob = [nt(kv[o, 1], og_i) for o in range(REACH + 1)]
        delta = functools.reduce(
            jnp.add,
            [
                jnp.sum(halves[o].astype(F32) * dprob[o], axis=0, keepdims=True)
                for o in range(REACH + 1)
            ],
        )
        dq = jnp.zeros((DIM, tok), F32)
        for o in range(REACH + 1):
            ds = (probs[o] * (dprob[o] - delta)).astype(BF16)
            dacc[o, 0] += nn(ds, q_i)
            dacc[o, 1] += nn(halves[o], og_i)
            dq += nn(kt[o], ds)
        gq_ref[:, cols(i)] = (jnp.transpose(dq) * SCALE).astype(BF16)
        return 0

    lax.fori_loop(0, q_heads // 2, attend, 0)

    for which in (0, 1):
        st_copies[which, 1].wait_recv()
        base_at = 1 - lax.rem(pos[which], 2)

        def reach_loop(h, _, which=which, base_at=base_at):
            st_out[which, 2, h] = (
                factor(which, 2, h) * st_out[which, base_at, h].astype(F32)
                + factor(which, 3, h) * st_in[which, 1, h].astype(F32)
            ).astype(BF16)
            return 0

        lax.fori_loop(0, heads, reach_loop, 0)
        send_state(which, 2)

    lax.fori_loop(q_heads // 2, q_heads, attend, 0)

    dkv_copies = {}
    for d in (4, 2, 3, 1):
        dkv_out[d - 1, 0] = (dacc[d, 0] * SCALE).astype(BF16)
        dkv_out[d - 1, 1] = dacc[d, 1].astype(BF16)
        dkv_copies[d] = push(
            dkv_out.at[d - 1],
            dkv_in.at[d - 1],
            dkv_send.at[d - 1],
            dkv_recv.at[d - 1],
            (seq_at(-d), hd),
        )
        dkv_copies[d].start()

    for which in (0, 1):
        st_copies[which, 2].wait_recv()

    def arrived(which, h):
        return (
            factor(which, 4, h) * st_in[which, 0, h].astype(F32)
            + factor(which, 5, h) * st_in[which, 1, h].astype(F32)
            + factor(which, 6, h) * st_in[which, 2, h].astype(F32)
        ).astype(BF16)

    def carry_loop(h, sums):
        state, adjoint = arrived(0, h), arrived(1, h)
        x_h = x_ref[:, cols(h)]
        g_h = g_ref[:, cols(h)]
        tail_h, lead_h = tail_col[h], lead_col[h]
        gi_ref[:, cols(h)] = (gi_acc[:, cols(h)] + nn(w_ref[...], adjoint) * tail_h).astype(BF16)
        return (
            sums[0] + nt(x_h, adjoint) * tail_h,
            sums[1] + nt(g_h, state) * lead_h,
        )

    zeros = jnp.zeros((tok, DIM), F32)
    gw, gr = lax.fori_loop(0, heads, carry_loop, (zeros, zeros))
    rows_each = tok // n_head
    for c in range(n_head):
        tot[c, 0] += gw[c * rows_each : (c + 1) * rows_each]
        tot[c, 1] += gr[c * rows_each : (c + 1) * rows_each]
    rs_copies = []
    for p in range(1, n_head):
        to = head_at(p)
        copy = push(tot.at[to], rs_in.at[p - 1], rs_send.at[p - 1], rs_recv.at[p - 1], (me, to))
        copy.start()
        rs_copies.append(copy)

    gk = dacc[0, 0] * SCALE
    gv = dacc[0, 1]
    for d in (4, 2, 3, 1):
        dkv_copies[d].wait_recv()
        gk += dkv_in[d - 1, 0].astype(F32)
        gv += dkv_in[d - 1, 1].astype(F32)
    gk_ref[...] = gk.astype(BF16)
    gv_ref[...] = gv.astype(BF16)

    gw_out = tot[hd, 0]
    gr_out = tot[hd, 1]
    for p in range(1, n_head):
        rs_copies[p - 1].wait_recv()
        gw_out += rs_in[p - 1, 0]
        gr_out += rs_in[p - 1, 1]
    gw_ref[...] = gw_out
    gr_ref[...] = gr_out

    for copy in kv_copies.values():
        copy.wait_send()
    for copy in c_copies:
        copy.wait_send()
    for copy in st_copies.values():
        copy.wait_send()
    for copy in dkv_copies.values():
        copy.wait_send()
    for copy in rs_copies:
        copy.wait_send()


def on_device(n_seq, n_head, *args):
    (x, g, w, r, step, rate, gain, q, k, v, og, docs) = args
    tok, heads = x.shape[0], step.shape[0]
    vmem = pl.BlockSpec(memory_space=pltpu.VMEM)
    smem = pl.BlockSpec(memory_space=pltpu.SMEM)
    rows_each = tok // n_head
    dma = pltpu.SemaphoreType.DMA
    scratch = [
        pltpu.VMEM((REACH + 1, 2, tok, DIM), BF16),
        pltpu.VMEM((REACH + 1, DIM, tok), BF16),
        pltpu.VMEM((REACH + 1, 2, tok, DIM), F32),
        pltpu.VMEM((REACH, 2, tok, DIM), BF16),
        pltpu.VMEM((REACH, 2, tok, DIM), BF16),
        pltpu.VMEM((7, heads, DIM), F32),
        pltpu.VMEM((2, 3, heads, DIM, DIM), BF16),
        pltpu.VMEM((2, 3, heads, DIM, DIM), BF16),
        pltpu.VMEM((DIM, tok), F32),
        pltpu.VMEM((DIM, tok), F32),
        pltpu.VMEM((3, heads, tok), F32),
        pltpu.VMEM((heads, tok, 1), F32),
        pltpu.VMEM((heads, tok, 1), F32),
        pltpu.VMEM((heads, tok, 1), F32),
        pltpu.VMEM((tok, heads * DIM), F32),
        pltpu.VMEM((tok, tok), F32),
        pltpu.VMEM((2, 7, heads, DIM), F32),
        pltpu.VMEM((n_head, 2, rows_each, DIM), F32),
        pltpu.VMEM((n_head - 1, 2, rows_each, DIM), F32),
        dma((REACH,)),
        dma((REACH,)),
        dma((6,)),
        dma((7,)),
        dma((2, 3)),
        dma((2, 3)),
        dma((REACH,)),
        dma((REACH,)),
        dma((n_head - 1,)),
        dma((n_head - 1,)),
    ]
    return pl.pallas_call(
        functools.partial(kernel, n_seq, n_head),
        out_shape=(
            jax.ShapeDtypeStruct(x.shape, BF16),
            jax.ShapeDtypeStruct((rows_each, DIM), F32),
            jax.ShapeDtypeStruct((rows_each, DIM), F32),
            jax.ShapeDtypeStruct(q.shape, BF16),
            jax.ShapeDtypeStruct(k.shape, BF16),
            jax.ShapeDtypeStruct(v.shape, BF16),
        ),
        in_specs=[vmem] * 5 + [smem] * 2 + [vmem] * 5,
        out_specs=(vmem,) * 6,
        scratch_shapes=scratch,
        compiler_params=pltpu.CompilerParams(
            collective_id=0, has_side_effects=True, vmem_limit_bytes=48 * 2**20
        ),
    )(x, g, w, r, step, rate, gain, q, k, v, og, docs.reshape(1, -1))


def solution(mesh):
    placed = (
        P("seq", "head"),
        P("seq", "head"),
        P("seq", None),
        P("seq", None),
        P("head", "seq"),
        P("head"),
        P("head"),
        P("seq", "head"),
        P("seq", "head"),
        P("seq", "head"),
        P("seq", "head"),
        P(),
    )
    return jax.shard_map(
        functools.partial(on_device, mesh.shape["seq"], mesh.shape["head"]),
        mesh=mesh,
        in_specs=placed,
        out_specs=(
            P("seq", "head"),
            P(("seq", "head"), None),
            P(("seq", "head"), None),
            P("seq", "head"),
            P("seq", "head"),
            P("seq", "head"),
        ),
        check_vma=False,
    )
```

```python
import functools
import math

import jax
import jax.numpy as jnp
from jax import lax
from jax.experimental import pallas as pl
from jax.experimental.pallas import tpu as pltpu
from jax.sharding import PartitionSpec as P

MESH = pl.DeviceIdType.MESH
REACH = 4
DIM = 128
NEG = -1e30
SCALE = DIM ** (-0.5)
SCALE2 = SCALE * math.log2(math.e)
SHIFT = 1
CHUNKS = 4
KV_ROW = True

F32 = jnp.float32
BF16 = jnp.bfloat16


def nn(a, b):
    return jnp.dot(a, b, preferred_element_type=F32)


def nt(a, b):
    return lax.dot_general(a, b, (((1,), (1,)), ((), ())), preferred_element_type=F32)


def flip(a):
    return jnp.transpose(a.astype(F32))


def cols(h):
    return pl.ds(pl.multiple_of(h * DIM, DIM), DIM)


def kernel(
    n_seq,
    n_head,
    x_hbm,
    g_hbm,
    w_hbm,
    r_hbm,
    step_hbm,
    rate_hbm,
    gain_hbm,
    q_hbm,
    k_hbm,
    v_hbm,
    og_hbm,
    doc_hbm,
    gi_ref,
    gw_ref,
    gr_ref,
    gq_ref,
    gk_ref,
    gv_ref,
    x_ref,
    g_ref,
    w_ref,
    r_ref,
    step_ref,
    rate_ref,
    gain_ref,
    q_ref,
    og_ref,
    doc_ref,
    kv,
    kt,
    q_rows,
    og_rows,
    ds_all,
    ph_all,
    own_grad,
    dkv_out,
    dkv_in,
    cbuf,
    st_out,
    st_in,
    wt,
    rt,
    rows,
    run_col,
    tail_col,
    lead_col,
    gi_acc,
    w_acc,
    coef,
    tot,
    rs_out,
    rs_in,
    load_sem,
    kv_send,
    kv_recv,
    c_send,
    c_recv,
    st_send,
    st_recv,
    dkv_send,
    dkv_recv,
    rs_send,
    rs_recv,
):
    tok = x_ref.shape[0]
    heads = step_ref.shape[0]
    q_heads = q_ref.shape[1] // DIM
    me = lax.axis_index("seq")
    hd = lax.axis_index("head")

    def seq_at(d):
        return lax.rem(me + (d + n_seq), n_seq)

    def head_at(p):
        return lax.rem(hd + p, n_head)

    def push(src, dst, send, recv, to):
        return pltpu.make_async_remote_copy(
            src_ref=src, dst_ref=dst, send_sem=send, recv_sem=recv, device_id=to, device_id_type=MESH
        )

    barrier = pltpu.get_barrier_semaphore()
    offsets = [d for d in range(-REACH, REACH + 1) if d]
    for d in offsets:
        pl.semaphore_signal(barrier, inc=1, device_id=(seq_at(d), hd), device_id_type=MESH)
    for p in range(1, n_head):
        pl.semaphore_signal(barrier, inc=1, device_id=(me, head_at(p)), device_id_type=MESH)

    loads = {}
    for i, (name, src, dst) in enumerate(
        (
            ("k", k_hbm, kv.at[0, 0]),
            ("v", v_hbm, kv.at[0, 1]),
            ("doc", doc_hbm, doc_ref),
            ("rate", rate_hbm, rate_ref),
            ("step", step_hbm, step_ref),
            ("w", w_hbm, w_ref),
            ("r", r_hbm, r_ref),
            ("x", x_hbm, x_ref),
            ("g", g_hbm, g_ref),
            ("gain", gain_hbm, gain_ref),
            ("q", q_hbm, q_ref),
            ("og", og_hbm, og_ref),
        )
    ):
        loads[name] = pltpu.make_async_copy(src, dst, load_sem.at[i])
        loads[name].start()

    def loaded(*which):
        for name in which:
            loads[name].wait()

    loaded("k", "v")
    pl.semaphore_wait(barrier, len(offsets) + n_head - 1)

    lane = lax.rem(me, 4)
    kv_copies = {4: push(kv.at[0], kv.at[4], kv_send.at[3], kv_recv.at[3], (seq_at(4), hd))}
    kv_copies[4].start()
    for d in (1, 3, 2):
        wraps = lane + d >= 4
        if KV_ROW:
            source = jnp.where(wraps, 4, 0)
            to = me - lane + lax.rem(lane + d, 4)
        else:
            source, to = 0, seq_at(d)
        copy = push(kv.at[source], kv.at[d], kv_send.at[d - 1], kv_recv.at[d - 1], (to, hd))
        kv_copies[d] = copy
        if KV_ROW:
            pl.when(jnp.logical_not(wraps))(copy.start)
        else:
            copy.start()

    loaded("doc", "rate", "step")
    base = (me * tok).astype(F32)
    lens = jnp.broadcast_to(doc_ref[...].astype(F32), (DIM, DIM))
    i0 = lax.broadcasted_iota(jnp.int32, (DIM, DIM), 0)
    i1 = lax.broadcasted_iota(jnp.int32, (DIM, DIM), 1)
    first_c = jnp.sum(jnp.where(i1 < i0, lens, 0.0), axis=1, keepdims=True)
    lens_c = jnp.sum(jnp.where(i1 == i0, lens, 0.0), axis=1, keepdims=True)
    first_r = jnp.sum(jnp.where(i0 < i1, lens_c, 0.0), axis=0, keepdims=True)
    t_row = base + lax.broadcasted_iota(jnp.int32, (1, tok), 1).astype(F32)
    t_col = base + lax.broadcasted_iota(jnp.int32, (tok, 1), 0).astype(F32)
    fp_row = jnp.max(jnp.where(first_c <= t_row, first_c, 0.0), axis=0, keepdims=True)
    fp_col = jnp.max(jnp.where(first_r <= t_col, first_r, 0.0), axis=1, keepdims=True)
    fp_last = fp_row[:, tok - 1 : tok]

    on_diag = lax.broadcasted_iota(jnp.int32, (heads, heads), 0) == lax.broadcasted_iota(
        jnp.int32, (heads, heads), 1
    )
    rate = jnp.sum(jnp.where(on_diag, rate_ref[...], 0.0), axis=1, keepdims=True)
    decay = -(rate * step_ref[...])
    j0 = lax.broadcasted_iota(jnp.int32, (tok, tok), 0)
    j1 = lax.broadcasted_iota(jnp.int32, (tok, tok), 1)
    run_r = jnp.dot(
        decay,
        (j0 <= j1).astype(F32),
        preferred_element_type=F32,
        precision=lax.Precision.HIGHEST,
    )
    run_c = lax.dot_general(
        (j1 <= j0).astype(F32),
        decay,
        (((1,), (1,)), ((), ())),
        preferred_element_type=F32,
        precision=lax.Precision.HIGHEST,
    )
    total_c = run_r[:, tok - 1 : tok]
    total_r = run_c[tok - 1 : tok, :]
    rows[0] = run_r
    rows[1] = jnp.where(fp_row == fp_last, jnp.exp(total_c - run_r), 0.0)
    rows[2] = jnp.where(fp_row < base, jnp.exp(run_r), 0.0)
    cbuf[3] = jnp.broadcast_to(jnp.where(fp_last < base, jnp.exp(total_c), 0.0), (heads, DIM))
    c_copies = []
    for i, d in enumerate((-3, -2, -1, 1, 2, 3)):
        copy = push(cbuf.at[3], cbuf.at[3 - d], c_send.at[i], c_recv.at[3 - d], (seq_at(d), hd))
        copy.start()
        c_copies.append(copy)

    loaded("w", "r", "x", "g")
    wt[...] = flip(w_ref[...])
    rt[...] = flip(r_ref[...])

    pos = (lax.rem(me, 4), lax.rem(3 + SHIFT + n_seq - me, 4))
    sign = (1, -1)
    each = heads // CHUNKS

    def state_copy(which, stage, c):
        y = pos[which]
        step = (1 - 2 * lax.rem(y, 2), 3 - 2 * y, 4)[stage]
        to = lax.rem(me + sign[which] * step + n_seq, n_seq)
        part = pl.ds(c * each, each)
        return push(
            st_out.at[which, stage, part],
            st_in.at[which, stage, part],
            st_send.at[which, stage, c],
            st_recv.at[which, stage, c],
            (to, hd),
        )

    def part_loop(c, _):
        for k in range(each):
            h = c * each + k
            scaled_w = (wt[...] * rows[1, pl.ds(h, 1), :]).astype(BF16)
            scaled_r = (rt[...] * rows[2, pl.ds(h, 1), :]).astype(BF16)
            st_out[0, 0, h] = nn(scaled_w, x_ref[:, cols(h)]).astype(BF16)
            st_out[1, 0, h] = nn(scaled_r, g_ref[:, cols(h)]).astype(BF16)
        for which in (0, 1):
            state_copy(which, 0, c).start()
        return 0

    lax.fori_loop(0, CHUNKS, part_loop, 0)

    tail_c = jnp.where(fp_col == fp_last, jnp.exp(total_r - run_c), 0.0)
    lead_c = jnp.where(fp_col < base, jnp.exp(run_c), 0.0)
    for h in range(heads):
        run_col[h] = run_c[:, h : h + 1]
        tail_col[h] = tail_c[:, h : h + 1]
        lead_col[h] = lead_c[:, h : h + 1]

    cross = nt(w_ref[...], r_ref[...])
    loaded("gain", "q", "og")
    head_lane = lax.broadcasted_iota(jnp.int32, (1, heads), 1)
    keep = (j0 <= j1) & (fp_col == fp_row)
    w_acc[...] = jnp.zeros_like(w_acc)

    def local_loop(h, _):
        x_h = x_ref[:, cols(h)]
        g_h = g_ref[:, cols(h)]
        corr = nt(x_h, g_h)
        dec = jnp.exp(jnp.where(keep, rows[0, pl.ds(h, 1), :] - run_col[h], NEG))
        w_acc[...] += corr * dec
        gain = jnp.sum(jnp.where(head_lane == h, gain_ref[...], 0.0), axis=1, keepdims=True)
        mix = (cross * dec).astype(BF16)
        gi_acc[:, cols(h)] = nn(mix, g_h) + gain * g_h.astype(F32)
        return 0

    lax.fori_loop(0, heads, local_loop, 0)
    w_sum = w_acc[...]
    gw = nn(w_sum.astype(BF16), r_ref[...])
    gr = nn(flip(w_sum).astype(BF16), w_ref[...])
    for c in range(n_head):
        tot[c, 0] = gw[c * (tok // n_head) : (c + 1) * (tok // n_head)]
        tot[c, 1] = gr[c * (tok // n_head) : (c + 1) * (tok // n_head)]

    if KV_ROW:
        kv_copies[4].wait_recv()
        for d in (1, 3, 2):
            pl.when(lane + d >= 4)(kv_copies[d].start)

    for copy in c_copies:
        copy.wait_recv()
    for which in (0, 1):
        y, s = pos[which], sign[which]
        c0, c1, c2, c3 = [cbuf[3 + s * (q - y)] for q in range(4)]
        own, after = cbuf[3], cbuf[3 + s]
        odd = lax.rem(y, 2) == 1
        one, zero = jnp.ones_like(own), jnp.zeros_like(own)
        coef[which, 0] = jnp.where(odd, one, after)
        coef[which, 1] = jnp.where(odd, own, one)
        coef[which, 2] = jnp.where(y < 2, c2 * c3, one)
        coef[which, 3] = jnp.where(y < 2, one, zero)
        coef[which, 4] = jnp.where(odd, one, zero)
        coef[which, 5] = jnp.where(y == 2, one, jnp.where(y == 3, c2, zero))
        coef[which, 6] = jnp.where(
            y == 0, one, jnp.where(y == 1, c0, jnp.where(y == 2, c0 * c1, c0 * c1 * c2))
        )

    def factor(which, i, h):
        return coef[which, i, pl.ds(h, 1), :]

    def pair_loop(c, _):
        for which in (0, 1):
            state_copy(which, 0, c).wait_recv()
            for k in range(each):
                h = c * each + k
                st_out[which, 1, h] = (
                    factor(which, 0, h) * st_out[which, 0, h].astype(F32)
                    + factor(which, 1, h) * st_in[which, 0, h].astype(F32)
                ).astype(BF16)
            state_copy(which, 1, c).start()
        return 0

    lax.fori_loop(0, CHUNKS, pair_loop, 0)

    for i in range(q_heads):
        q_rows[i * tok : (i + 1) * tok] = q_ref[:, i * DIM : (i + 1) * DIM]
        og_rows[i * tok : (i + 1) * tok] = og_ref[:, i * DIM : (i + 1) * DIM]
    for d in (1, 3, 2) if KV_ROW else (4, 1, 3, 2):
        kv_copies[d].wait_recv()
    for o in range(REACH + 1):
        kt[o] = flip(kv[o, 0]).astype(BF16)
    spot = lax.broadcasted_iota(jnp.int32, (tok, 1), 0).astype(F32)

    def attend(i):
        q_i = q_ref[:, cols(i)]
        og_i = og_ref[:, cols(i)]
        here = pl.ds(pl.multiple_of(i * tok, tok), tok)
        scores = []
        for o in range(REACH + 1):
            key_pos = spot + (base - float(o * tok))
            allowed = key_pos >= fp_row
            if o == 0:
                allowed = allowed & (key_pos <= t_row)
            scores.append(jnp.where(allowed, nt(kv[o, 0], q_i) * SCALE2, NEG))
        top = functools.reduce(jnp.maximum, [jnp.max(s, axis=0, keepdims=True) for s in scores])
        weights = [jnp.exp2(s - top) for s in scores]
        norm = 1.0 / functools.reduce(
            jnp.add, [jnp.sum(e, axis=0, keepdims=True) for e in weights]
        )
        probs = [e * norm for e in weights]
        halves = [p.astype(BF16) for p in probs]
        dprob = [nt(kv[o, 1], og_i) for o in range(REACH + 1)]
        delta = functools.reduce(
            jnp.add,
            [
                jnp.sum(halves[o].astype(F32) * dprob[o], axis=0, keepdims=True)
                for o in range(REACH + 1)
            ],
        )
        dq = jnp.zeros((DIM, tok), F32)
        for o in range(REACH + 1):
            ds = (probs[o] * (dprob[o] - delta)).astype(BF16)
            ds_all[o, :, here] = ds
            ph_all[o, :, here] = halves[o]
            dq += nn(kt[o], ds)
        gq_ref[:, cols(i)] = (jnp.transpose(dq) * SCALE).astype(BF16)

    def attend_loop(c, _):
        attend(c)
        for which in (0, 1):
            state_copy(which, 1, c).wait_recv()
            first = 1 - lax.rem(pos[which], 2)
            for k in range(each):
                h = c * each + k
                st_out[which, 2, h] = (
                    factor(which, 2, h) * st_out[which, first, h].astype(F32)
                    + factor(which, 3, h) * st_in[which, 1, h].astype(F32)
                ).astype(BF16)
            state_copy(which, 2, c).start()
        return 0

    lax.fori_loop(0, CHUNKS, attend_loop, 0)

    def dkv_copy(d):
        return push(
            dkv_out.at[d - 1],
            dkv_in.at[d - 1],
            dkv_send.at[d - 1],
            dkv_recv.at[d - 1],
            (lax.rem(me - d + n_seq, n_seq), hd),
        )

    def grad_loop(step, _):
        d = REACH - step
        dkv_out[d - 1, 0] = (nn(ds_all[d], q_rows[...]) * SCALE).astype(BF16)
        dkv_out[d - 1, 1] = nn(ph_all[d], og_rows[...]).astype(BF16)
        dkv_copy(d).start()
        return 0

    lax.fori_loop(0, REACH, grad_loop, 0)
    own_grad[0] = nn(ds_all[0], q_rows[...]) * SCALE
    own_grad[1] = nn(ph_all[0], og_rows[...])

    def arrived(which, h):
        return (
            factor(which, 4, h) * st_in[which, 0, h].astype(F32)
            + factor(which, 5, h) * st_in[which, 1, h].astype(F32)
            + factor(which, 6, h) * st_in[which, 2, h].astype(F32)
        ).astype(BF16)

    def carry_loop(c, sums):
        gw, gr = sums
        for which in (0, 1):
            state_copy(which, 2, c).wait_recv()
        for k in range(each):
            h = c * each + k
            state, adjoint = arrived(0, h), arrived(1, h)
            x_h = x_ref[:, cols(h)]
            g_h = g_ref[:, cols(h)]
            tail_h, lead_h = tail_col[h], lead_col[h]
            gi_ref[:, cols(h)] = (
                gi_acc[:, cols(h)] + nn(w_ref[...], adjoint) * tail_h
            ).astype(BF16)
            gw += nt(x_h, adjoint) * tail_h
            gr += nt(g_h, state) * lead_h
        return gw, gr

    zeros = jnp.zeros((tok, DIM), F32)
    gw, gr = lax.fori_loop(0, CHUNKS, carry_loop, (zeros, zeros))
    rows_each = tok // n_head
    for c in range(n_head):
        for i, total in enumerate((gw, gr)):
            part = tot[c, i] + total[c * rows_each : (c + 1) * rows_each]
            tot[c, i] = part
            rs_out[c, i] = part.astype(BF16)
    rs_copies = []
    for p in range(1, n_head):
        to = head_at(p)
        copy = push(rs_out.at[to], rs_in.at[p - 1], rs_send.at[p - 1], rs_recv.at[p - 1], (me, to))
        copy.start()
        rs_copies.append(copy)

    gk, gv = own_grad[0], own_grad[1]
    for d in (4, 3, 2, 1):
        dkv_copy(d).wait_recv()
        gk += dkv_in[d - 1, 0].astype(F32)
        gv += dkv_in[d - 1, 1].astype(F32)
    gk_ref[...] = gk.astype(BF16)
    gv_ref[...] = gv.astype(BF16)

    gw_out = tot[hd, 0]
    gr_out = tot[hd, 1]
    for p in range(1, n_head):
        rs_copies[p - 1].wait_recv()
        gw_out += rs_in[p - 1, 0].astype(F32)
        gr_out += rs_in[p - 1, 1].astype(F32)
    gw_ref[...] = gw_out
    gr_ref[...] = gr_out

    for copy in kv_copies.values():
        copy.wait_send()
    for copy in c_copies:
        copy.wait_send()

    def drain(c, _):
        for which in (0, 1):
            for stage in range(3):
                state_copy(which, stage, c).wait_send()
        dkv_copy(c + 1).wait_send()
        return 0

    lax.fori_loop(0, CHUNKS, drain, 0)
    for copy in rs_copies:
        copy.wait_send()


def store(*refs):
    *refs, sem = refs
    count = len(refs) // 2
    copies = [
        pltpu.make_async_copy(refs[i], refs[count + i], sem.at[i]) for i in range(count)
    ]
    for copy in copies:
        copy.start()
    for copy in copies:
        copy.wait()


def on_device(n_seq, n_head, *args):
    (x, g, w, r, step, rate, gain, q, k, v, og, docs) = args
    tok, heads = x.shape[0], step.shape[0]
    vmem = pl.BlockSpec(memory_space=pltpu.VMEM)
    hbm = pl.BlockSpec(memory_space=pltpu.HBM)
    rows_each = tok // n_head
    dma = pltpu.SemaphoreType.DMA
    scratch = [
        pltpu.VMEM(x.shape, BF16),
        pltpu.VMEM(g.shape, BF16),
        pltpu.VMEM(w.shape, BF16),
        pltpu.VMEM(r.shape, BF16),
        pltpu.VMEM(step.shape, F32),
        pltpu.VMEM((1, heads), F32),
        pltpu.VMEM((1, heads), F32),
        pltpu.VMEM(q.shape, BF16),
        pltpu.VMEM(og.shape, BF16),
        pltpu.VMEM((1, docs.shape[0]), jnp.int32),
        pltpu.VMEM((REACH + 1, 2, tok, DIM), BF16),
        pltpu.VMEM((REACH + 1, DIM, tok), BF16),
        pltpu.VMEM((q.shape[1] // DIM * tok, DIM), BF16),
        pltpu.VMEM((q.shape[1] // DIM * tok, DIM), BF16),
        pltpu.VMEM((REACH + 1, tok, q.shape[1] // DIM * tok), BF16),
        pltpu.VMEM((REACH + 1, tok, q.shape[1] // DIM * tok), BF16),
        pltpu.VMEM((2, tok, DIM), F32),
        pltpu.VMEM((REACH, 2, tok, DIM), BF16),
        pltpu.VMEM((REACH, 2, tok, DIM), BF16),
        pltpu.VMEM((7, heads, DIM), F32),
        pltpu.VMEM((2, 3, heads, DIM, DIM), BF16),
        pltpu.VMEM((2, 3, heads, DIM, DIM), BF16),
        pltpu.VMEM((DIM, tok), F32),
        pltpu.VMEM((DIM, tok), F32),
        pltpu.VMEM((3, heads, tok), F32),
        pltpu.VMEM((heads, tok, 1), F32),
        pltpu.VMEM((heads, tok, 1), F32),
        pltpu.VMEM((heads, tok, 1), F32),
        pltpu.VMEM((tok, heads * DIM), F32),
        pltpu.VMEM((tok, tok), F32),
        pltpu.VMEM((2, 7, heads, DIM), F32),
        pltpu.VMEM((n_head, 2, rows_each, DIM), F32),
        pltpu.VMEM((n_head, 2, rows_each, DIM), BF16),
        pltpu.VMEM((n_head - 1, 2, rows_each, DIM), BF16),
        dma((len(args),)),
        dma((REACH,)),
        dma((REACH,)),
        dma((6,)),
        dma((7,)),
        dma((2, 3, CHUNKS)),
        dma((2, 3, CHUNKS)),
        dma((REACH,)),
        dma((REACH,)),
        dma((n_head - 1,)),
        dma((n_head - 1,)),
    ]
    made = pl.pallas_call(
        functools.partial(kernel, n_seq, n_head),
        out_shape=(
            jax.ShapeDtypeStruct(x.shape, BF16),
            jax.ShapeDtypeStruct((rows_each, DIM), F32),
            jax.ShapeDtypeStruct((rows_each, DIM), F32),
            jax.ShapeDtypeStruct(q.shape, BF16),
            jax.ShapeDtypeStruct(k.shape, BF16),
            jax.ShapeDtypeStruct(v.shape, BF16),
        ),
        in_specs=[hbm] * len(args),
        out_specs=(vmem,) * 6,
        scratch_shapes=scratch,
        compiler_params=pltpu.CompilerParams(
            collective_id=0, has_side_effects=True, vmem_limit_bytes=48 * 2**20
        ),
    )(*[pltpu.with_memory_space_constraint(a, pltpu.HBM) for a in (x, g, w, r, step, rate.reshape(1, -1), gain.reshape(1, -1), q, k, v, og, docs.reshape(1, -1))])
    return pl.pallas_call(
        store,
        out_shape=[jax.ShapeDtypeStruct(m.shape, m.dtype) for m in made],
        in_specs=[vmem] * len(made),
        out_specs=[hbm] * len(made),
        scratch_shapes=[dma((len(made),))],
        compiler_params=pltpu.CompilerParams(vmem_limit_bytes=2 * 2**20),
    )(*made)


def solution(mesh):
    placed = (
        P("seq", "head"),
        P("seq", "head"),
        P("seq", None),
        P("seq", None),
        P("head", "seq"),
        P("head"),
        P("head"),
        P("seq", "head"),
        P("seq", "head"),
        P("seq", "head"),
        P("seq", "head"),
        P(),
    )
    return jax.shard_map(
        functools.partial(on_device, mesh.shape["seq"], mesh.shape["head"]),
        mesh=mesh,
        in_specs=placed,
        out_specs=(
            P("seq", "head"),
            P(("seq", "head"), None),
            P(("seq", "head"), None),
            P("seq", "head"),
            P("seq", "head"),
            P("seq", "head"),
        ),
        check_vma=False,
    )
```

```python
import functools
import math

import jax
import jax.numpy as jnp
from jax import lax
from jax.experimental import pallas as pl
from jax.experimental.pallas import tpu as pltpu
from jax.sharding import PartitionSpec as P

MESH = pl.DeviceIdType.MESH
REACH = 4
DIM = 128
NEG = -1e30
SCALE = DIM ** (-0.5)
SCALE2 = SCALE * math.log2(math.e)
CHUNKS = 4
ORDER = 0

F32 = jnp.float32
BF16 = jnp.bfloat16


def nn(a, b):
    return jnp.dot(a, b, preferred_element_type=F32)


def nt(a, b):
    return lax.dot_general(a, b, (((1,), (1,)), ((), ())), preferred_element_type=F32)


def flip(a):
    return jnp.transpose(a.astype(F32))


def cols(h):
    return pl.ds(pl.multiple_of(h * DIM, DIM), DIM)


def kernel(
    n_seq,
    n_head,
    x_hbm,
    g_hbm,
    w_hbm,
    r_hbm,
    step_hbm,
    rate_hbm,
    gain_hbm,
    q_hbm,
    k_hbm,
    v_hbm,
    og_hbm,
    doc_hbm,
    gi_ref,
    gw_ref,
    gr_ref,
    gq_ref,
    gk_ref,
    gv_ref,
    x_ref,
    g_ref,
    w_ref,
    r_ref,
    step_ref,
    rate_ref,
    gain_ref,
    q_ref,
    og_ref,
    doc_ref,
    kv,
    kt,
    q_rows,
    og_rows,
    s_all,
    dp_all,
    row_norm,
    row_delta,
    dq_acc,
    ds_all,
    ph_all,
    own_grad,
    dkv_out,
    dkv_in,
    cbuf,
    st_out,
    st_in,
    wt,
    rt,
    rows,
    run_col,
    tail_col,
    lead_col,
    gi_acc,
    w_acc,
    coef,
    tot,
    rs_out,
    rs_in,
    load_sem,
    kv_send,
    kv_recv,
    c_send,
    c_recv,
    st_send,
    st_recv,
    dkv_send,
    dkv_recv,
    rs_send,
    rs_recv,
):
    tok = x_ref.shape[0]
    heads = step_ref.shape[0]
    q_heads = q_ref.shape[1] // DIM
    me = lax.axis_index("seq")
    hd = lax.axis_index("head")

    def seq_at(d):
        return lax.rem(me + (d + n_seq), n_seq)

    def exists(d):
        return (me + d >= 0) & (me + d < n_seq)

    def absent(d):
        return jnp.logical_not(exists(d))

    def head_at(p):
        return lax.rem(hd + p, n_head)

    def push(src, dst, send, recv, to):
        return pltpu.make_async_remote_copy(
            src_ref=src, dst_ref=dst, send_sem=send, recv_sem=recv, device_id=to, device_id_type=MESH
        )

    barrier = pltpu.get_barrier_semaphore()
    offsets = [d for d in range(-REACH, REACH + 1) if d]
    peers = n_head - 1
    for d in offsets:
        there = exists(d)
        peers += there.astype(jnp.int32)

        @pl.when(there)
        def _(d=d):
            pl.semaphore_signal(barrier, inc=1, device_id=(seq_at(d), hd), device_id_type=MESH)

    for p in range(1, n_head):
        pl.semaphore_signal(barrier, inc=1, device_id=(me, head_at(p)), device_id_type=MESH)

    loads = {}
    for i, (name, src, dst) in enumerate(
        (
            ("k", k_hbm, kv.at[0, 0]),
            ("v", v_hbm, kv.at[0, 1]),
            ("doc", doc_hbm, doc_ref),
            ("rate", rate_hbm, rate_ref),
            ("step", step_hbm, step_ref),
            ("w", w_hbm, w_ref),
            ("r", r_hbm, r_ref),
            ("x", x_hbm, x_ref),
            ("g", g_hbm, g_ref),
            ("gain", gain_hbm, gain_ref),
            ("q", q_hbm, q_ref),
            ("og", og_hbm, og_ref),
        )
    ):
        loads[name] = pltpu.make_async_copy(src, dst, load_sem.at[i])
        loads[name].start()

    def loaded(*which):
        for name in which:
            loads[name].wait()

    loaded("doc", "rate", "step")
    base = (me * tok).astype(F32)
    lens = jnp.broadcast_to(doc_ref[...].astype(F32), (DIM, DIM))
    i0 = lax.broadcasted_iota(jnp.int32, (DIM, DIM), 0)
    i1 = lax.broadcasted_iota(jnp.int32, (DIM, DIM), 1)
    first_c = jnp.sum(jnp.where(i1 < i0, lens, 0.0), axis=1, keepdims=True)
    lens_c = jnp.sum(jnp.where(i1 == i0, lens, 0.0), axis=1, keepdims=True)
    first_r = jnp.sum(jnp.where(i0 < i1, lens_c, 0.0), axis=0, keepdims=True)
    t_row = base + lax.broadcasted_iota(jnp.int32, (1, tok), 1).astype(F32)
    t_col = base + lax.broadcasted_iota(jnp.int32, (tok, 1), 0).astype(F32)
    fp_row = jnp.max(jnp.where(first_c <= t_row, first_c, 0.0), axis=0, keepdims=True)
    fp_col = jnp.max(jnp.where(first_r <= t_col, first_r, 0.0), axis=1, keepdims=True)
    fp_last = fp_row[:, tok - 1 : tok]

    on_diag = lax.broadcasted_iota(jnp.int32, (heads, heads), 0) == lax.broadcasted_iota(
        jnp.int32, (heads, heads), 1
    )
    rate = jnp.sum(jnp.where(on_diag, rate_ref[...], 0.0), axis=1, keepdims=True)
    decay = -(rate * step_ref[...])
    j0 = lax.broadcasted_iota(jnp.int32, (tok, tok), 0)
    j1 = lax.broadcasted_iota(jnp.int32, (tok, tok), 1)
    run_r = jnp.dot(
        decay,
        (j0 <= j1).astype(F32),
        preferred_element_type=F32,
        precision=lax.Precision.HIGHEST,
    )
    run_c = lax.dot_general(
        (j1 <= j0).astype(F32),
        decay,
        (((1,), (1,)), ((), ())),
        preferred_element_type=F32,
        precision=lax.Precision.HIGHEST,
    )
    total_c = run_r[:, tok - 1 : tok]
    total_r = run_c[tok - 1 : tok, :]
    rows[0] = run_r
    rows[1] = jnp.where(fp_row == fp_last, jnp.exp(total_c - run_r), 0.0)
    rows[2] = jnp.where(fp_row < base, jnp.exp(run_r), 0.0)
    cbuf[3] = jnp.broadcast_to(jnp.where(fp_last < base, jnp.exp(total_c), 0.0), (heads, DIM))

    loaded("k", "v")
    pl.semaphore_wait(barrier, peers)
    kv_copies = {}
    for d in (4, 1, 3, 2):
        kv_copies[d] = push(
            kv.at[0], kv.at[d], kv_send.at[d - 1], kv_recv.at[d - 1], (seq_at(d), hd)
        )
        pl.when(exists(d))(kv_copies[d].start)
    c_copies = {}
    for d in (-3, -2, -1, 1, 2, 3):
        c_copies[d] = push(
            cbuf.at[3], cbuf.at[3 - d], c_send.at[d + 3], c_recv.at[3 - d], (seq_at(d), hd)
        )
        pl.when(exists(d))(c_copies[d].start)

        @pl.when(absent(d))
        def _(d=d):
            cbuf[3 + d] = jnp.zeros_like(cbuf[3 + d])

    for d in range(1, REACH + 1):

        @pl.when(absent(-d))
        def _(d=d):
            kv[d] = jnp.zeros_like(kv[d])

        @pl.when(absent(d))
        def _(d=d):
            dkv_in[d - 1] = jnp.zeros_like(dkv_in[d - 1])

    parity = lax.rem(me, 2)
    later = (parity == 1, parity == 0)
    sign = (1, -1)
    ahead = [jnp.where(later[w], sign[w], 3 * sign[w]) for w in (0, 1)]
    behind = [jnp.where(later[w], -3 * sign[w], -sign[w]) for w in (0, 1)]
    sends = [(None, exists(ahead[w]), exists(4 * sign[w])) for w in (0, 1)]
    gets = [(None, exists(behind[w]), exists(-4 * sign[w])) for w in (0, 1)]

    def when(condition, do):
        if condition is None:
            do()
        else:
            pl.when(condition)(do)

    for which in (0, 1):
        for stage in (1, 2):

            @pl.when(jnp.logical_not(gets[which][stage]))
            def _(which=which, stage=stage):
                st_in[which, stage] = jnp.zeros_like(st_in[which, stage])

    loaded("w", "r", "x", "g")
    wt[...] = flip(w_ref[...])
    rt[...] = flip(r_ref[...])

    each = heads // CHUNKS

    def state_copy(which, stage, c):
        step = (1 - 2 * parity, ahead[which], 4 * sign[which])[stage]
        source = (0, 1, jnp.where(later[which], 0, 1))[stage]
        part = pl.ds(c * each, each)
        return push(
            st_out.at[which, source, part],
            st_in.at[which, stage, part],
            st_send.at[which, stage, c],
            st_recv.at[which, stage, c],
            (lax.rem(me + step + n_seq, n_seq), hd),
        )

    def part_loop(c, _):
        for k in range(each):
            h = c * each + k
            scaled_w = (wt[...] * rows[1, pl.ds(h, 1), :]).astype(BF16)
            scaled_r = (rt[...] * rows[2, pl.ds(h, 1), :]).astype(BF16)
            st_out[0, 0, h] = nn(scaled_w, x_ref[:, cols(h)]).astype(BF16)
            st_out[1, 0, h] = nn(scaled_r, g_ref[:, cols(h)]).astype(BF16)
        for which in (0, 1):
            state_copy(which, 0, c).start()
            pl.when(later[which] & sends[which][2])(state_copy(which, 2, c).start)
        return 0

    lax.fori_loop(0, CHUNKS, part_loop, 0)

    tail_c = jnp.where(fp_col == fp_last, jnp.exp(total_r - run_c), 0.0)
    lead_c = jnp.where(fp_col < base, jnp.exp(run_c), 0.0)
    for h in range(heads):
        run_col[h] = run_c[:, h : h + 1]
        tail_col[h] = tail_c[:, h : h + 1]
        lead_col[h] = lead_c[:, h : h + 1]

    cross = nt(w_ref[...], r_ref[...])
    loaded("gain", "q", "og")
    head_lane = lax.broadcasted_iota(jnp.int32, (1, heads), 1)
    keep = (j0 <= j1) & (fp_col == fp_row)
    w_acc[...] = jnp.zeros_like(w_acc)

    def local_loop(h, _):
        x_h = x_ref[:, cols(h)]
        g_h = g_ref[:, cols(h)]
        corr = nt(x_h, g_h)
        dec = jnp.exp(jnp.where(keep, rows[0, pl.ds(h, 1), :] - run_col[h], NEG))
        w_acc[...] += corr * dec
        gain = jnp.sum(jnp.where(head_lane == h, gain_ref[...], 0.0), axis=1, keepdims=True)
        mix = (cross * dec).astype(BF16)
        gi_acc[:, cols(h)] = nn(mix, g_h) + gain * g_h.astype(F32)
        return 0

    lax.fori_loop(0, heads, local_loop, 0)
    for d, copy in c_copies.items():
        pl.when(exists(-d))(copy.wait_recv)
    for which in (0, 1):
        s = sign[which]
        c1, c2, c3 = [cbuf[3 - s * k] for k in (1, 2, 3)]
        own, partner = cbuf[3], cbuf[3 + s]
        one, zero = jnp.ones_like(own), jnp.zeros_like(own)
        coef[which, 0] = jnp.where(later[which], one, partner)
        coef[which, 1] = jnp.where(later[which], own, one)
        coef[which, 2] = jnp.where(later[which], one, zero)
        coef[which, 3] = jnp.where(later[which], c1, one)
        coef[which, 4] = jnp.where(later[which], c1 * c2 * c3, c1 * c2)

    def factor(which, i, h):
        return coef[which, i, pl.ds(h, 1), :]

    def pair_step(c, _=0):
        for which in (0, 1):
            state_copy(which, 0, c).wait_recv()
            for k in range(each):
                h = c * each + k
                st_out[which, 1, h] = (
                    factor(which, 0, h) * st_out[which, 0, h].astype(F32)
                    + factor(which, 1, h) * st_in[which, 0, h].astype(F32)
                ).astype(BF16)
            when(sends[which][1], state_copy(which, 1, c).start)
            pl.when(jnp.logical_not(later[which]) & sends[which][2])(state_copy(which, 2, c).start)
        return 0

    for i in range(q_heads):
        q_rows[i * tok : (i + 1) * tok] = q_ref[:, i * DIM : (i + 1) * DIM]
        og_rows[i * tok : (i + 1) * tok] = og_ref[:, i * DIM : (i + 1) * DIM]
    spot = lax.broadcasted_iota(jnp.int32, (tok, 1), 0).astype(F32)

    def head_lanes(i):
        return pl.ds(pl.multiple_of(i * tok, tok), tok)

    def score_step(o):
        kt[o] = flip(kv[o, 0]).astype(BF16)

        def one_head(i, _):
            key_pos = spot + (base - float(o * tok))
            allowed = key_pos >= fp_row
            if o == 0:
                allowed = allowed & (key_pos <= t_row)
            s_all[o, :, head_lanes(i)] = jnp.where(
                allowed, nt(kv[o, 0], q_ref[:, cols(i)]) * SCALE2, NEG
            )
            dp_all[o, :, head_lanes(i)] = nt(kv[o, 1], og_ref[:, cols(i)])
            return 0

        lax.fori_loop(0, q_heads, one_head, 0)

    def softmax_step(i):
        here = head_lanes(i)
        blocks = range(REACH + 1)
        scores = [s_all[o, :, here] for o in blocks]
        top = functools.reduce(jnp.maximum, [jnp.max(s, axis=0, keepdims=True) for s in scores])
        weights = [jnp.exp2(s - top) for s in scores]
        for o in blocks:
            s_all[o, :, here] = weights[o]
        norm = 1.0 / functools.reduce(
            jnp.add, [jnp.sum(e, axis=0, keepdims=True) for e in weights]
        )
        row_norm[:, here] = norm
        row_delta[:, here] = norm * functools.reduce(
            jnp.add,
            [jnp.sum(weights[o] * dp_all[o, :, here], axis=0, keepdims=True) for o in blocks],
        )

    def grad_step(d):
        def one_head(i, _):
            here = head_lanes(i)
            prob = s_all[d, :, here] * row_norm[:, here]
            ds = (prob * (dp_all[d, :, here] - row_delta[:, here])).astype(BF16)
            ds_all[d, :, here] = ds
            ph_all[d, :, here] = prob.astype(BF16)
            dq_acc[i] += nn(kt[d], ds)
            return 0

        lax.fori_loop(0, q_heads, one_head, 0)

    def kv_step(d):
        pl.when(exists(-d))(kv_copies[d].wait_recv)
        score_step(d)

    score_step(0)
    for d, c in zip((4, 1, 3, 2), range(CHUNKS)):
        if ORDER == 0:
            pair_step(c)
            kv_step(d)
        elif ORDER == 1:
            kv_step(d)
            pair_step(c)
        elif ORDER == 2:
            if c < 2:
                pair_step(2 * c)
                pair_step(2 * c + 1)
            kv_step(d)
        else:
            kv_step(d)
            if c >= 2:
                pair_step(2 * c - 4)
                pair_step(2 * c - 3)

    def attend_loop(c, _):
        softmax_step(c)
        return 0

    dq_acc[...] = jnp.zeros_like(dq_acc)

    lax.fori_loop(0, CHUNKS, attend_loop, 0)

    def dkv_copy(d):
        return push(
            dkv_out.at[d - 1],
            dkv_in.at[d - 1],
            dkv_send.at[d - 1],
            dkv_recv.at[d - 1],
            (lax.rem(me - d + n_seq, n_seq), hd),
        )

    def grad_loop(step, _):
        d = REACH - step
        grad_step(d)
        dkv_out[d - 1, 0] = (nn(ds_all[d], q_rows[...]) * SCALE).astype(BF16)
        dkv_out[d - 1, 1] = nn(ph_all[d], og_rows[...]).astype(BF16)
        pl.when(me >= d)(dkv_copy(d).start)
        return 0

    lax.fori_loop(0, REACH, grad_loop, 0)
    grad_step(0)
    for i in range(q_heads):
        gq_ref[:, i * DIM : (i + 1) * DIM] = (jnp.transpose(dq_acc[i]) * SCALE).astype(BF16)
    own_grad[0] = nn(ds_all[0], q_rows[...]) * SCALE
    own_grad[1] = nn(ph_all[0], og_rows[...])
    w_sum = w_acc[...]
    gw = nn(w_sum.astype(BF16), r_ref[...])
    gr = nn(flip(w_sum).astype(BF16), w_ref[...])
    for c in range(n_head):
        tot[c, 0] = gw[c * (tok // n_head) : (c + 1) * (tok // n_head)]
        tot[c, 1] = gr[c * (tok // n_head) : (c + 1) * (tok // n_head)]

    def arrived(which, h):
        return (
            factor(which, 2, h) * st_in[which, 0, h].astype(F32)
            + factor(which, 3, h) * st_in[which, 1, h].astype(F32)
            + factor(which, 4, h) * st_in[which, 2, h].astype(F32)
        ).astype(BF16)

    def carry_loop(c, sums):
        gw, gr = sums
        for which in (0, 1):
            for stage in (1, 2):
                pl.when(gets[which][stage])(state_copy(which, stage, c).wait_recv)
        for k in range(each):
            h = c * each + k
            state, adjoint = arrived(0, h), arrived(1, h)
            x_h = x_ref[:, cols(h)]
            g_h = g_ref[:, cols(h)]
            tail_h, lead_h = tail_col[h], lead_col[h]
            gi_ref[:, cols(h)] = (
                gi_acc[:, cols(h)] + nn(w_ref[...], adjoint) * tail_h
            ).astype(BF16)
            gw += nt(x_h, adjoint) * tail_h
            gr += nt(g_h, state) * lead_h
        return gw, gr

    zeros = jnp.zeros((tok, DIM), F32)
    gw, gr = lax.fori_loop(0, CHUNKS, carry_loop, (zeros, zeros))
    rows_each = tok // n_head
    for c in range(n_head):
        for i, total in enumerate((gw, gr)):
            part = tot[c, i] + total[c * rows_each : (c + 1) * rows_each]
            tot[c, i] = part
            rs_out[c, i] = part.astype(BF16)
    rs_copies = []
    for p in range(1, n_head):
        to = head_at(p)
        copy = push(rs_out.at[to], rs_in.at[p - 1], rs_send.at[p - 1], rs_recv.at[p - 1], (me, to))
        copy.start()
        rs_copies.append(copy)

    gk, gv = own_grad[0], own_grad[1]
    for d in (4, 3, 2, 1):
        pl.when(exists(d))(dkv_copy(d).wait_recv)
        gk += dkv_in[d - 1, 0].astype(F32)
        gv += dkv_in[d - 1, 1].astype(F32)
    gk_ref[...] = gk.astype(BF16)
    gv_ref[...] = gv.astype(BF16)

    gw_out = tot[hd, 0]
    gr_out = tot[hd, 1]
    for p in range(1, n_head):
        rs_copies[p - 1].wait_recv()
        gw_out += rs_in[p - 1, 0].astype(F32)
        gr_out += rs_in[p - 1, 1].astype(F32)
    gw_ref[...] = gw_out
    gr_ref[...] = gr_out

    for d, copy in kv_copies.items():
        pl.when(exists(d))(copy.wait_send)
    for d, copy in c_copies.items():
        pl.when(exists(d))(copy.wait_send)

    def drain(c, _):
        for which in (0, 1):
            for stage in range(3):
                when(sends[which][stage], state_copy(which, stage, c).wait_send)
        pl.when(me > c)(dkv_copy(c + 1).wait_send)
        return 0

    lax.fori_loop(0, CHUNKS, drain, 0)

    for copy in rs_copies:
        copy.wait_send()


def store(*refs):
    *refs, sem = refs
    count = len(refs) // 2
    copies = [
        pltpu.make_async_copy(refs[i], refs[count + i], sem.at[i]) for i in range(count)
    ]
    for copy in copies:
        copy.start()
    for copy in copies:
        copy.wait()


def on_device(n_seq, n_head, *args):
    (x, g, w, r, step, rate, gain, q, k, v, og, docs) = args
    tok, heads = x.shape[0], step.shape[0]
    vmem = pl.BlockSpec(memory_space=pltpu.VMEM)
    hbm = pl.BlockSpec(memory_space=pltpu.HBM)
    rows_each = tok // n_head
    dma = pltpu.SemaphoreType.DMA
    scratch = [
        pltpu.VMEM(x.shape, BF16),
        pltpu.VMEM(g.shape, BF16),
        pltpu.VMEM(w.shape, BF16),
        pltpu.VMEM(r.shape, BF16),
        pltpu.VMEM(step.shape, F32),
        pltpu.VMEM((1, heads), F32),
        pltpu.VMEM((1, heads), F32),
        pltpu.VMEM(q.shape, BF16),
        pltpu.VMEM(og.shape, BF16),
        pltpu.VMEM((1, docs.shape[0]), jnp.int32),
        pltpu.VMEM((REACH + 1, 2, tok, DIM), BF16),
        pltpu.VMEM((REACH + 1, DIM, tok), BF16),
        pltpu.VMEM((q.shape[1] // DIM * tok, DIM), BF16),
        pltpu.VMEM((q.shape[1] // DIM * tok, DIM), BF16),
        pltpu.VMEM((REACH + 1, tok, q.shape[1] // DIM * tok), F32),
        pltpu.VMEM((REACH + 1, tok, q.shape[1] // DIM * tok), F32),
        pltpu.VMEM((1, q.shape[1] // DIM * tok), F32),
        pltpu.VMEM((1, q.shape[1] // DIM * tok), F32),
        pltpu.VMEM((q.shape[1] // DIM, DIM, tok), F32),
        pltpu.VMEM((REACH + 1, tok, q.shape[1] // DIM * tok), BF16),
        pltpu.VMEM((REACH + 1, tok, q.shape[1] // DIM * tok), BF16),
        pltpu.VMEM((2, tok, DIM), F32),
        pltpu.VMEM((REACH, 2, tok, DIM), BF16),
        pltpu.VMEM((REACH, 2, tok, DIM), BF16),
        pltpu.VMEM((7, heads, DIM), F32),
        pltpu.VMEM((2, 2, heads, DIM, DIM), BF16),
        pltpu.VMEM((2, 3, heads, DIM, DIM), BF16),
        pltpu.VMEM((DIM, tok), F32),
        pltpu.VMEM((DIM, tok), F32),
        pltpu.VMEM((3, heads, tok), F32),
        pltpu.VMEM((heads, tok, 1), F32),
        pltpu.VMEM((heads, tok, 1), F32),
        pltpu.VMEM((heads, tok, 1), F32),
        pltpu.VMEM((tok, heads * DIM), F32),
        pltpu.VMEM((tok, tok), F32),
        pltpu.VMEM((2, 5, heads, DIM), F32),
        pltpu.VMEM((n_head, 2, rows_each, DIM), F32),
        pltpu.VMEM((n_head, 2, rows_each, DIM), BF16),
        pltpu.VMEM((n_head - 1, 2, rows_each, DIM), BF16),
        dma((len(args),)),
        dma((REACH,)),
        dma((REACH,)),
        dma((7,)),
        dma((7,)),
        dma((2, 3, CHUNKS)),
        dma((2, 3, CHUNKS)),
        dma((REACH,)),
        dma((REACH,)),
        dma((n_head - 1,)),
        dma((n_head - 1,)),
    ]
    made = pl.pallas_call(
        functools.partial(kernel, n_seq, n_head),
        out_shape=(
            jax.ShapeDtypeStruct(x.shape, BF16),
            jax.ShapeDtypeStruct((rows_each, DIM), F32),
            jax.ShapeDtypeStruct((rows_each, DIM), F32),
            jax.ShapeDtypeStruct(q.shape, BF16),
            jax.ShapeDtypeStruct(k.shape, BF16),
            jax.ShapeDtypeStruct(v.shape, BF16),
        ),
        in_specs=[hbm] * len(args),
        out_specs=(vmem,) * 6,
        scratch_shapes=scratch,
        compiler_params=pltpu.CompilerParams(
            collective_id=0, has_side_effects=True, vmem_limit_bytes=48 * 2**20
        ),
    )(*[pltpu.with_memory_space_constraint(a, pltpu.HBM) for a in (x, g, w, r, step, rate.reshape(1, -1), gain.reshape(1, -1), q, k, v, og, docs.reshape(1, -1))])
    return pl.pallas_call(
        store,
        out_shape=[jax.ShapeDtypeStruct(m.shape, m.dtype) for m in made],
        in_specs=[vmem] * len(made),
        out_specs=[hbm] * len(made),
        scratch_shapes=[dma((len(made),))],
        compiler_params=pltpu.CompilerParams(vmem_limit_bytes=2 * 2**20),
    )(*made)


def solution(mesh):
    placed = (
        P("seq", "head"),
        P("seq", "head"),
        P("seq", None),
        P("seq", None),
        P("head", "seq"),
        P("head"),
        P("head"),
        P("seq", "head"),
        P("seq", "head"),
        P("seq", "head"),
        P("seq", "head"),
        P(),
    )
    return jax.shard_map(
        functools.partial(on_device, mesh.shape["seq"], mesh.shape["head"]),
        mesh=mesh,
        in_specs=placed,
        out_specs=(
            P("seq", "head"),
            P(("seq", "head"), None),
            P(("seq", "head"), None),
            P("seq", "head"),
            P("seq", "head"),
            P("seq", "head"),
        ),
        check_vma=False,
    )
```

```python
import functools
import math

import jax
import jax.numpy as jnp
from jax import lax
from jax.experimental import pallas as pl
from jax.experimental.pallas import tpu as pltpu
from jax.sharding import PartitionSpec as P

MESH = pl.DeviceIdType.MESH
REACH = 4
DIM = 128
NEG = -1e30
SCALE = DIM ** (-0.5)
SCALE2 = SCALE * math.log2(math.e)
CHUNKS = 4

F32 = jnp.float32
BF16 = jnp.bfloat16


def nn(a, b):
    return jnp.dot(a, b, preferred_element_type=F32)


def nt(a, b):
    return lax.dot_general(a, b, (((1,), (1,)), ((), ())), preferred_element_type=F32)


def flip(a):
    return jnp.transpose(a.astype(F32))


def cols(h):
    return pl.ds(pl.multiple_of(h * DIM, DIM), DIM)


def kernel(
    n_seq,
    n_head,
    x_hbm,
    g_hbm,
    w_hbm,
    r_hbm,
    step_hbm,
    rate_hbm,
    gain_hbm,
    q_hbm,
    k_hbm,
    v_hbm,
    og_hbm,
    doc_hbm,
    gi_ref,
    gw_ref,
    gr_ref,
    gq_ref,
    gk_ref,
    gv_ref,
    x_ref,
    g_ref,
    w_ref,
    r_ref,
    step_ref,
    rate_ref,
    gain_ref,
    q_ref,
    og_ref,
    doc_ref,
    kv,
    kt,
    q_rows,
    og_rows,
    s_all,
    dp_all,
    row_norm,
    row_delta,
    dq_acc,
    ds_all,
    ph_all,
    own_grad,
    dkv_out,
    dkv_in,
    cbuf,
    st_out,
    st_in,
    wt,
    rt,
    rows,
    run_col,
    tail_col,
    lead_col,
    gi_acc,
    w_acc,
    coef,
    tot,
    rs_out,
    rs_in,
    load_sem,
    kv_send,
    kv_recv,
    c_send,
    c_recv,
    st_send,
    st_recv,
    dkv_send,
    dkv_recv,
    rs_send,
    rs_recv,
):
    tok = x_ref.shape[0]
    heads = step_ref.shape[0]
    q_heads = q_ref.shape[1] // DIM
    me = lax.axis_index("seq")
    hd = lax.axis_index("head")

    def seq_at(d):
        return lax.rem(me + (d + n_seq), n_seq)

    def exists(d):
        return (me + d >= 0) & (me + d < n_seq)

    def absent(d):
        return jnp.logical_not(exists(d))

    def head_at(p):
        return lax.rem(hd + p, n_head)

    def push(src, dst, send, recv, to):
        return pltpu.make_async_remote_copy(
            src_ref=src, dst_ref=dst, send_sem=send, recv_sem=recv, device_id=to, device_id_type=MESH
        )

    barrier = pltpu.get_barrier_semaphore()
    offsets = [d for d in range(-REACH, REACH + 1) if d]
    peers = n_head - 1
    for d in offsets:
        there = exists(d)
        peers += there.astype(jnp.int32)

        @pl.when(there)
        def _(d=d):
            pl.semaphore_signal(barrier, inc=1, device_id=(seq_at(d), hd), device_id_type=MESH)

    for p in range(1, n_head):
        pl.semaphore_signal(barrier, inc=1, device_id=(me, head_at(p)), device_id_type=MESH)

    loads = {}
    for i, (name, src, dst) in enumerate(
        (
            ("k", k_hbm, kv.at[0, 0]),
            ("v", v_hbm, kv.at[0, 1]),
            ("doc", doc_hbm, doc_ref),
            ("rate", rate_hbm, rate_ref),
            ("step", step_hbm, step_ref),
            ("w", w_hbm, w_ref),
            ("r", r_hbm, r_ref),
            ("x", x_hbm, x_ref),
            ("g", g_hbm, g_ref),
            ("gain", gain_hbm, gain_ref),
            ("q", q_hbm, q_ref),
            ("og", og_hbm, og_ref),
        )
    ):
        loads[name] = pltpu.make_async_copy(src, dst, load_sem.at[i])
        loads[name].start()

    def loaded(*which):
        for name in which:
            loads[name].wait()

    loaded("doc", "rate", "step")
    base = (me * tok).astype(F32)
    lens = jnp.broadcast_to(doc_ref[...].astype(F32), (DIM, DIM))
    i0 = lax.broadcasted_iota(jnp.int32, (DIM, DIM), 0)
    i1 = lax.broadcasted_iota(jnp.int32, (DIM, DIM), 1)
    first_c = jnp.sum(jnp.where(i1 < i0, lens, 0.0), axis=1, keepdims=True)
    lens_c = jnp.sum(jnp.where(i1 == i0, lens, 0.0), axis=1, keepdims=True)
    first_r = jnp.sum(jnp.where(i0 < i1, lens_c, 0.0), axis=0, keepdims=True)
    t_row = base + lax.broadcasted_iota(jnp.int32, (1, tok), 1).astype(F32)
    t_col = base + lax.broadcasted_iota(jnp.int32, (tok, 1), 0).astype(F32)
    fp_row = jnp.max(jnp.where(first_c <= t_row, first_c, 0.0), axis=0, keepdims=True)
    fp_col = jnp.max(jnp.where(first_r <= t_col, first_r, 0.0), axis=1, keepdims=True)
    fp_last = fp_row[:, tok - 1 : tok]

    on_diag = lax.broadcasted_iota(jnp.int32, (heads, heads), 0) == lax.broadcasted_iota(
        jnp.int32, (heads, heads), 1
    )
    rate = jnp.sum(jnp.where(on_diag, rate_ref[...], 0.0), axis=1, keepdims=True)
    decay = -(rate * step_ref[...])
    j0 = lax.broadcasted_iota(jnp.int32, (tok, tok), 0)
    j1 = lax.broadcasted_iota(jnp.int32, (tok, tok), 1)
    run_r = jnp.dot(
        decay,
        (j0 <= j1).astype(F32),
        preferred_element_type=F32,
        precision=lax.Precision.HIGHEST,
    )
    run_c = lax.dot_general(
        (j1 <= j0).astype(F32),
        decay,
        (((1,), (1,)), ((), ())),
        preferred_element_type=F32,
        precision=lax.Precision.HIGHEST,
    )
    total_c = run_r[:, tok - 1 : tok]
    total_r = run_c[tok - 1 : tok, :]
    rows[0] = run_r
    rows[1] = jnp.where(fp_row == fp_last, jnp.exp(total_c - run_r), 0.0)
    rows[2] = jnp.where(fp_row < base, jnp.exp(run_r), 0.0)
    cbuf[3] = jnp.broadcast_to(jnp.where(fp_last < base, jnp.exp(total_c), 0.0), (heads, DIM))

    loaded("k", "v")
    pl.semaphore_wait(barrier, peers)
    kv_copies = {}
    for d in (4, 1, 3, 2):
        kv_copies[d] = push(
            kv.at[0], kv.at[d], kv_send.at[d - 1], kv_recv.at[d - 1], (seq_at(d), hd)
        )
        pl.when(exists(d))(kv_copies[d].start)
    c_copies = {}
    for d in (-3, -2, -1, 1, 2, 3):
        c_copies[d] = push(
            cbuf.at[3], cbuf.at[3 - d], c_send.at[d + 3], c_recv.at[3 - d], (seq_at(d), hd)
        )
        pl.when(exists(d))(c_copies[d].start)

        @pl.when(absent(d))
        def _(d=d):
            cbuf[3 + d] = jnp.zeros_like(cbuf[3 + d])

    for d in range(1, REACH + 1):

        @pl.when(absent(-d))
        def _(d=d):
            kv[d] = jnp.zeros_like(kv[d])

        @pl.when(absent(d))
        def _(d=d):
            dkv_in[d - 1] = jnp.zeros_like(dkv_in[d - 1])

    parity = lax.rem(me, 2)
    later = (parity == 1, parity == 0)
    sign = (1, -1)
    ahead = [jnp.where(later[w], sign[w], 3 * sign[w]) for w in (0, 1)]
    behind = [jnp.where(later[w], -3 * sign[w], -sign[w]) for w in (0, 1)]
    sends = [(None, exists(ahead[w]), exists(4 * sign[w])) for w in (0, 1)]
    gets = [(None, exists(behind[w]), exists(-4 * sign[w])) for w in (0, 1)]

    def when(condition, do):
        if condition is None:
            do()
        else:
            pl.when(condition)(do)

    for which in (0, 1):
        for stage in (1, 2):

            @pl.when(jnp.logical_not(gets[which][stage]))
            def _(which=which, stage=stage):
                st_in[which, stage] = jnp.zeros_like(st_in[which, stage])

    loaded("w", "r", "x", "g")
    wt[...] = flip(w_ref[...])
    rt[...] = flip(r_ref[...])

    each = heads // CHUNKS

    def state_copy(which, stage, c):
        step = (1 - 2 * parity, ahead[which], 4 * sign[which])[stage]
        source = (0, 1, jnp.where(later[which], 0, 1))[stage]
        part = pl.ds(c * each, each)
        return push(
            st_out.at[which, source, part],
            st_in.at[which, stage, part],
            st_send.at[which, stage, c],
            st_recv.at[which, stage, c],
            (lax.rem(me + step + n_seq, n_seq), hd),
        )

    def part_loop(c, _):
        for k in range(each):
            h = c * each + k
            scaled_w = (wt[...] * rows[1, pl.ds(h, 1), :]).astype(BF16)
            scaled_r = (rt[...] * rows[2, pl.ds(h, 1), :]).astype(BF16)
            st_out[0, 0, h] = nn(scaled_w, x_ref[:, cols(h)]).astype(BF16)
            st_out[1, 0, h] = nn(scaled_r, g_ref[:, cols(h)]).astype(BF16)
        for which in (0, 1):
            state_copy(which, 0, c).start()
            pl.when(later[which] & sends[which][2])(state_copy(which, 2, c).start)
        return 0

    lax.fori_loop(0, CHUNKS, part_loop, 0)

    tail_c = jnp.where(fp_col == fp_last, jnp.exp(total_r - run_c), 0.0)
    lead_c = jnp.where(fp_col < base, jnp.exp(run_c), 0.0)
    for h in range(heads):
        run_col[h] = run_c[:, h : h + 1]
        tail_col[h] = tail_c[:, h : h + 1]
        lead_col[h] = lead_c[:, h : h + 1]

    cross = nt(w_ref[...], r_ref[...])
    loaded("gain", "q", "og")
    head_lane = lax.broadcasted_iota(jnp.int32, (1, heads), 1)
    keep = (j0 <= j1) & (fp_col == fp_row)
    w_acc[...] = jnp.zeros_like(w_acc)

    def local_loop(h, _):
        x_h = x_ref[:, cols(h)]
        g_h = g_ref[:, cols(h)]
        corr = nt(x_h, g_h)
        dec = jnp.exp(jnp.where(keep, rows[0, pl.ds(h, 1), :] - run_col[h], NEG))
        w_acc[...] += corr * dec
        gain = jnp.sum(jnp.where(head_lane == h, gain_ref[...], 0.0), axis=1, keepdims=True)
        mix = (cross * dec).astype(BF16)
        gi_acc[:, cols(h)] = nn(mix, g_h) + gain * g_h.astype(F32)
        return 0

    lax.fori_loop(0, heads, local_loop, 0)
    for d, copy in c_copies.items():
        pl.when(exists(-d))(copy.wait_recv)
    for which in (0, 1):
        s = sign[which]
        c1, c2, c3 = [cbuf[3 - s * k] for k in (1, 2, 3)]
        own, partner = cbuf[3], cbuf[3 + s]
        one, zero = jnp.ones_like(own), jnp.zeros_like(own)
        coef[which, 0] = jnp.where(later[which], one, partner)
        coef[which, 1] = jnp.where(later[which], own, one)
        coef[which, 2] = jnp.where(later[which], one, zero)
        coef[which, 3] = jnp.where(later[which], c1, one)
        coef[which, 4] = jnp.where(later[which], c1 * c2 * c3, c1 * c2)

    def factor(which, i, h):
        return coef[which, i, pl.ds(h, 1), :]

    def pair_step(c, _=0):
        for which in (0, 1):
            state_copy(which, 0, c).wait_recv()
            for k in range(each):
                h = c * each + k
                st_out[which, 1, h] = (
                    factor(which, 0, h) * st_out[which, 0, h].astype(F32)
                    + factor(which, 1, h) * st_in[which, 0, h].astype(F32)
                ).astype(BF16)
            when(sends[which][1], state_copy(which, 1, c).start)
            pl.when(jnp.logical_not(later[which]) & sends[which][2])(state_copy(which, 2, c).start)
        return 0

    for i in range(q_heads):
        q_rows[i * tok : (i + 1) * tok] = q_ref[:, i * DIM : (i + 1) * DIM]
        og_rows[i * tok : (i + 1) * tok] = og_ref[:, i * DIM : (i + 1) * DIM]
    spot = lax.broadcasted_iota(jnp.int32, (tok, 1), 0).astype(F32)

    def head_lanes(i):
        return pl.ds(pl.multiple_of(i * tok, tok), tok)

    def score_step(o):
        kt[o] = flip(kv[o, 0]).astype(BF16)

        def one_head(i, _):
            key_pos = spot + (base - float(o * tok))
            allowed = key_pos >= fp_row
            if o == 0:
                allowed = allowed & (key_pos <= t_row)
            s_all[o, :, head_lanes(i)] = jnp.where(
                allowed, nt(kv[o, 0], q_ref[:, cols(i)]) * SCALE2, NEG
            )
            dp_all[o, :, head_lanes(i)] = nt(kv[o, 1], og_ref[:, cols(i)])
            return 0

        lax.fori_loop(0, q_heads, one_head, 0, unroll=True)

    def softmax_step(i):
        here = head_lanes(i)
        blocks = range(REACH + 1)
        scores = [s_all[o, :, here] for o in blocks]
        top = functools.reduce(jnp.maximum, [jnp.max(s, axis=0, keepdims=True) for s in scores])
        weights = [jnp.exp2(s - top) for s in scores]
        for o in blocks:
            s_all[o, :, here] = weights[o]
        norm = 1.0 / functools.reduce(
            jnp.add, [jnp.sum(e, axis=0, keepdims=True) for e in weights]
        )
        row_norm[:, here] = norm
        row_delta[:, here] = norm * functools.reduce(
            jnp.add,
            [jnp.sum(weights[o] * dp_all[o, :, here], axis=0, keepdims=True) for o in blocks],
        )

    def grad_step(d):
        def one_head(i, _):
            here = head_lanes(i)
            prob = s_all[d, :, here] * row_norm[:, here]
            ds = (prob * (dp_all[d, :, here] - row_delta[:, here])).astype(BF16)
            ds_all[d, :, here] = ds
            ph_all[d, :, here] = prob.astype(BF16)
            dq_acc[i] += nn(kt[d], ds)
            return 0

        lax.fori_loop(0, q_heads, one_head, 0, unroll=True)

    def kv_step(d):
        pl.when(exists(-d))(kv_copies[d].wait_recv)
        score_step(d)

    score_step(0)
    for d, c in zip((4, 1, 3, 2), range(CHUNKS)):
        pair_step(c)
        kv_step(d)

    def attend_loop(c, _):
        softmax_step(c)
        return 0

    dq_acc[...] = jnp.zeros_like(dq_acc)

    lax.fori_loop(0, CHUNKS, attend_loop, 0)

    def dkv_copy(d):
        return push(
            dkv_out.at[d - 1],
            dkv_in.at[d - 1],
            dkv_send.at[d - 1],
            dkv_recv.at[d - 1],
            (lax.rem(me - d + n_seq, n_seq), hd),
        )

    def grad_loop(step, _):
        d = REACH - step
        grad_step(d)
        dkv_out[d - 1, 0] = (nn(ds_all[d], q_rows[...]) * SCALE).astype(BF16)
        dkv_out[d - 1, 1] = nn(ph_all[d], og_rows[...]).astype(BF16)
        pl.when(me >= d)(dkv_copy(d).start)
        return 0

    lax.fori_loop(0, REACH, grad_loop, 0)
    grad_step(0)
    for i in range(q_heads):
        gq_ref[:, i * DIM : (i + 1) * DIM] = (jnp.transpose(dq_acc[i]) * SCALE).astype(BF16)
    own_grad[0] = nn(ds_all[0], q_rows[...]) * SCALE
    own_grad[1] = nn(ph_all[0], og_rows[...])
    w_sum = w_acc[...]
    gw = nn(w_sum.astype(BF16), r_ref[...])
    gr = nn(flip(w_sum).astype(BF16), w_ref[...])
    for c in range(n_head):
        tot[c, 0] = gw[c * (tok // n_head) : (c + 1) * (tok // n_head)]
        tot[c, 1] = gr[c * (tok // n_head) : (c + 1) * (tok // n_head)]

    def arrived(which, h):
        return (
            factor(which, 2, h) * st_in[which, 0, h].astype(F32)
            + factor(which, 3, h) * st_in[which, 1, h].astype(F32)
            + factor(which, 4, h) * st_in[which, 2, h].astype(F32)
        ).astype(BF16)

    def carry_loop(c, sums):
        gw, gr = sums
        for which in (0, 1):
            for stage in (1, 2):
                pl.when(gets[which][stage])(state_copy(which, stage, c).wait_recv)
        for k in range(each):
            h = c * each + k
            state, adjoint = arrived(0, h), arrived(1, h)
            x_h = x_ref[:, cols(h)]
            g_h = g_ref[:, cols(h)]
            tail_h, lead_h = tail_col[h], lead_col[h]
            gi_ref[:, cols(h)] = (
                gi_acc[:, cols(h)] + nn(w_ref[...], adjoint) * tail_h
            ).astype(BF16)
            gw += nt(x_h, adjoint) * tail_h
            gr += nt(g_h, state) * lead_h
        return gw, gr

    zeros = jnp.zeros((tok, DIM), F32)
    gw, gr = lax.fori_loop(0, CHUNKS, carry_loop, (zeros, zeros))
    rows_each = tok // n_head
    for c in range(n_head):
        for i, total in enumerate((gw, gr)):
            part = tot[c, i] + total[c * rows_each : (c + 1) * rows_each]
            tot[c, i] = part
            rs_out[c, i] = part.astype(BF16)
    rs_copies = []
    for p in range(1, n_head):
        to = head_at(p)
        copy = push(rs_out.at[to], rs_in.at[p - 1], rs_send.at[p - 1], rs_recv.at[p - 1], (me, to))
        copy.start()
        rs_copies.append(copy)

    gk, gv = own_grad[0], own_grad[1]
    for d in (4, 3, 2, 1):
        pl.when(exists(d))(dkv_copy(d).wait_recv)
        gk += dkv_in[d - 1, 0].astype(F32)
        gv += dkv_in[d - 1, 1].astype(F32)
    gk_ref[...] = gk.astype(BF16)
    gv_ref[...] = gv.astype(BF16)

    gw_out = tot[hd, 0]
    gr_out = tot[hd, 1]
    for p in range(1, n_head):
        rs_copies[p - 1].wait_recv()
        gw_out += rs_in[p - 1, 0].astype(F32)
        gr_out += rs_in[p - 1, 1].astype(F32)
    gw_ref[...] = gw_out
    gr_ref[...] = gr_out

    for d, copy in kv_copies.items():
        pl.when(exists(d))(copy.wait_send)
    for d, copy in c_copies.items():
        pl.when(exists(d))(copy.wait_send)

    def drain(c, _):
        for which in (0, 1):
            for stage in range(3):
                when(sends[which][stage], state_copy(which, stage, c).wait_send)
        pl.when(me > c)(dkv_copy(c + 1).wait_send)
        return 0

    lax.fori_loop(0, CHUNKS, drain, 0)

    for copy in rs_copies:
        copy.wait_send()


def store(*refs):
    *refs, sem = refs
    count = len(refs) // 2
    copies = [
        pltpu.make_async_copy(refs[i], refs[count + i], sem.at[i]) for i in range(count)
    ]
    for copy in copies:
        copy.start()
    for copy in copies:
        copy.wait()


def on_device(n_seq, n_head, *args):
    (x, g, w, r, step, rate, gain, q, k, v, og, docs) = args
    tok, heads = x.shape[0], step.shape[0]
    vmem = pl.BlockSpec(memory_space=pltpu.VMEM)
    hbm = pl.BlockSpec(memory_space=pltpu.HBM)
    rows_each = tok // n_head
    dma = pltpu.SemaphoreType.DMA
    scratch = [
        pltpu.VMEM(x.shape, BF16),
        pltpu.VMEM(g.shape, BF16),
        pltpu.VMEM(w.shape, BF16),
        pltpu.VMEM(r.shape, BF16),
        pltpu.VMEM(step.shape, F32),
        pltpu.VMEM((1, heads), F32),
        pltpu.VMEM((1, heads), F32),
        pltpu.VMEM(q.shape, BF16),
        pltpu.VMEM(og.shape, BF16),
        pltpu.VMEM((1, docs.shape[0]), jnp.int32),
        pltpu.VMEM((REACH + 1, 2, tok, DIM), BF16),
        pltpu.VMEM((REACH + 1, DIM, tok), BF16),
        pltpu.VMEM((q.shape[1] // DIM * tok, DIM), BF16),
        pltpu.VMEM((q.shape[1] // DIM * tok, DIM), BF16),
        pltpu.VMEM((REACH + 1, tok, q.shape[1] // DIM * tok), F32),
        pltpu.VMEM((REACH + 1, tok, q.shape[1] // DIM * tok), F32),
        pltpu.VMEM((1, q.shape[1] // DIM * tok), F32),
        pltpu.VMEM((1, q.shape[1] // DIM * tok), F32),
        pltpu.VMEM((q.shape[1] // DIM, DIM, tok), F32),
        pltpu.VMEM((REACH + 1, tok, q.shape[1] // DIM * tok), BF16),
        pltpu.VMEM((REACH + 1, tok, q.shape[1] // DIM * tok), BF16),
        pltpu.VMEM((2, tok, DIM), F32),
        pltpu.VMEM((REACH, 2, tok, DIM), BF16),
        pltpu.VMEM((REACH, 2, tok, DIM), BF16),
        pltpu.VMEM((7, heads, DIM), F32),
        pltpu.VMEM((2, 2, heads, DIM, DIM), BF16),
        pltpu.VMEM((2, 3, heads, DIM, DIM), BF16),
        pltpu.VMEM((DIM, tok), F32),
        pltpu.VMEM((DIM, tok), F32),
        pltpu.VMEM((3, heads, tok), F32),
        pltpu.VMEM((heads, tok, 1), F32),
        pltpu.VMEM((heads, tok, 1), F32),
        pltpu.VMEM((heads, tok, 1), F32),
        pltpu.VMEM((tok, heads * DIM), F32),
        pltpu.VMEM((tok, tok), F32),
        pltpu.VMEM((2, 5, heads, DIM), F32),
        pltpu.VMEM((n_head, 2, rows_each, DIM), F32),
        pltpu.VMEM((n_head, 2, rows_each, DIM), BF16),
        pltpu.VMEM((n_head - 1, 2, rows_each, DIM), BF16),
        dma((len(args),)),
        dma((REACH,)),
        dma((REACH,)),
        dma((7,)),
        dma((7,)),
        dma((2, 3, CHUNKS)),
        dma((2, 3, CHUNKS)),
        dma((REACH,)),
        dma((REACH,)),
        dma((n_head - 1,)),
        dma((n_head - 1,)),
    ]
    made = pl.pallas_call(
        functools.partial(kernel, n_seq, n_head),
        out_shape=(
            jax.ShapeDtypeStruct(x.shape, BF16),
            jax.ShapeDtypeStruct((rows_each, DIM), F32),
            jax.ShapeDtypeStruct((rows_each, DIM), F32),
            jax.ShapeDtypeStruct(q.shape, BF16),
            jax.ShapeDtypeStruct(k.shape, BF16),
            jax.ShapeDtypeStruct(v.shape, BF16),
        ),
        in_specs=[hbm] * len(args),
        out_specs=(vmem,) * 6,
        scratch_shapes=scratch,
        compiler_params=pltpu.CompilerParams(
            collective_id=0, has_side_effects=True, vmem_limit_bytes=48 * 2**20
        ),
    )(*[pltpu.with_memory_space_constraint(a, pltpu.HBM) for a in (x, g, w, r, step, rate.reshape(1, -1), gain.reshape(1, -1), q, k, v, og, docs.reshape(1, -1))])
    return pl.pallas_call(
        store,
        out_shape=[jax.ShapeDtypeStruct(m.shape, m.dtype) for m in made],
        in_specs=[vmem] * len(made),
        out_specs=[hbm] * len(made),
        scratch_shapes=[dma((len(made),))],
        compiler_params=pltpu.CompilerParams(vmem_limit_bytes=2 * 2**20),
    )(*made)


def solution(mesh):
    placed = (
        P("seq", "head"),
        P("seq", "head"),
        P("seq", None),
        P("seq", None),
        P("head", "seq"),
        P("head"),
        P("head"),
        P("seq", "head"),
        P("seq", "head"),
        P("seq", "head"),
        P("seq", "head"),
        P(),
    )
    return jax.shard_map(
        functools.partial(on_device, mesh.shape["seq"], mesh.shape["head"]),
        mesh=mesh,
        in_specs=placed,
        out_specs=(
            P("seq", "head"),
            P(("seq", "head"), None),
            P(("seq", "head"), None),
            P("seq", "head"),
            P("seq", "head"),
            P("seq", "head"),
        ),
        check_vma=False,
    )
```

```python
import functools
import math

import jax
import jax.numpy as jnp
from jax import lax
from jax.experimental import pallas as pl
from jax.experimental.pallas import tpu as pltpu
from jax.sharding import PartitionSpec as P

MESH = pl.DeviceIdType.MESH
REACH = 4
DIM = 128
NEG = -1e30
SCALE = DIM ** (-0.5)
SCALE2 = SCALE * math.log2(math.e)
CHUNKS = 4

F32 = jnp.float32
BF16 = jnp.bfloat16


def nn(a, b):
    return jnp.dot(a, b, preferred_element_type=F32)


def nt(a, b):
    return lax.dot_general(a, b, (((1,), (1,)), ((), ())), preferred_element_type=F32)


def flip(a):
    return jnp.transpose(a.astype(F32))


def cols(h):
    return pl.ds(pl.multiple_of(h * DIM, DIM), DIM)


def kernel(
    n_seq,
    n_head,
    x_hbm,
    g_hbm,
    w_hbm,
    r_hbm,
    step_hbm,
    rate_hbm,
    gain_hbm,
    q_hbm,
    k_hbm,
    v_hbm,
    og_hbm,
    doc_hbm,
    gi_ref,
    gw_ref,
    gr_ref,
    gq_ref,
    gk_ref,
    gv_ref,
    x_ref,
    g_ref,
    w_ref,
    r_ref,
    step_ref,
    rate_ref,
    gain_ref,
    q_ref,
    og_ref,
    doc_ref,
    kv,
    kt,
    q_rows,
    og_rows,
    s_all,
    dp_all,
    row_norm,
    row_delta,
    dq_acc,
    ds_all,
    ph_all,
    own_grad,
    dkv_out,
    dkv_in,
    cbuf,
    st_out,
    st_in,
    wt,
    rt,
    rows,
    run_col,
    tail_col,
    lead_col,
    gi_acc,
    w_acc,
    coef,
    tot,
    rs_out,
    rs_in,
    load_sem,
    kv_send,
    kv_recv,
    c_send,
    c_recv,
    st_send,
    st_recv,
    dkv_send,
    dkv_recv,
    rs_send,
    rs_recv,
):
    tok = x_ref.shape[0]
    heads = step_ref.shape[0]
    q_heads = q_ref.shape[1] // DIM
    me = lax.axis_index("seq")
    hd = lax.axis_index("head")

    def seq_at(d):
        return lax.rem(me + (d + n_seq), n_seq)

    def exists(d):
        return (me + d >= 0) & (me + d < n_seq)

    def absent(d):
        return jnp.logical_not(exists(d))

    def head_at(p):
        return lax.rem(hd + p, n_head)

    def push(src, dst, send, recv, to):
        return pltpu.make_async_remote_copy(
            src_ref=src, dst_ref=dst, send_sem=send, recv_sem=recv, device_id=to, device_id_type=MESH
        )

    barrier = pltpu.get_barrier_semaphore()
    offsets = [d for d in range(-REACH, REACH + 1) if d]
    peers = n_head - 1
    for d in offsets:
        there = exists(d)
        peers += there.astype(jnp.int32)

        @pl.when(there)
        def _(d=d):
            pl.semaphore_signal(barrier, inc=1, device_id=(seq_at(d), hd), device_id_type=MESH)

    for p in range(1, n_head):
        pl.semaphore_signal(barrier, inc=1, device_id=(me, head_at(p)), device_id_type=MESH)

    loads = {}
    for i, (name, src, dst) in enumerate(
        (
            ("k", k_hbm, kv.at[0, 0]),
            ("v", v_hbm, kv.at[0, 1]),
            ("doc", doc_hbm, doc_ref),
            ("rate", rate_hbm, rate_ref),
            ("step", step_hbm, step_ref),
            ("w", w_hbm, w_ref),
            ("r", r_hbm, r_ref),
            ("x", x_hbm, x_ref),
            ("g", g_hbm, g_ref),
            ("gain", gain_hbm, gain_ref),
            ("q", q_hbm, q_ref),
            ("og", og_hbm, og_ref),
        )
    ):
        loads[name] = pltpu.make_async_copy(src, dst, load_sem.at[i])
        loads[name].start()

    def loaded(*which):
        for name in which:
            loads[name].wait()

    loaded("doc", "rate", "step")
    base = (me * tok).astype(F32)
    lens = jnp.broadcast_to(doc_ref[...].astype(F32), (DIM, DIM))
    i0 = lax.broadcasted_iota(jnp.int32, (DIM, DIM), 0)
    i1 = lax.broadcasted_iota(jnp.int32, (DIM, DIM), 1)
    first_c = jnp.sum(jnp.where(i1 < i0, lens, 0.0), axis=1, keepdims=True)
    lens_c = jnp.sum(jnp.where(i1 == i0, lens, 0.0), axis=1, keepdims=True)
    first_r = jnp.sum(jnp.where(i0 < i1, lens_c, 0.0), axis=0, keepdims=True)
    t_row = base + lax.broadcasted_iota(jnp.int32, (1, tok), 1).astype(F32)
    t_col = base + lax.broadcasted_iota(jnp.int32, (tok, 1), 0).astype(F32)
    fp_row = jnp.max(jnp.where(first_c <= t_row, first_c, 0.0), axis=0, keepdims=True)
    fp_col = jnp.max(jnp.where(first_r <= t_col, first_r, 0.0), axis=1, keepdims=True)
    fp_last = fp_row[:, tok - 1 : tok]

    on_diag = lax.broadcasted_iota(jnp.int32, (heads, heads), 0) == lax.broadcasted_iota(
        jnp.int32, (heads, heads), 1
    )
    rate = jnp.sum(jnp.where(on_diag, rate_ref[...], 0.0), axis=1, keepdims=True)
    decay = -(rate * step_ref[...])
    j0 = lax.broadcasted_iota(jnp.int32, (tok, tok), 0)
    j1 = lax.broadcasted_iota(jnp.int32, (tok, tok), 1)
    run_r = jnp.dot(
        decay,
        (j0 <= j1).astype(F32),
        preferred_element_type=F32,
        precision=lax.Precision.HIGHEST,
    )
    run_c = lax.dot_general(
        (j1 <= j0).astype(F32),
        decay,
        (((1,), (1,)), ((), ())),
        preferred_element_type=F32,
        precision=lax.Precision.HIGHEST,
    )
    total_c = run_r[:, tok - 1 : tok]
    total_r = run_c[tok - 1 : tok, :]
    rows[0] = run_r
    rows[1] = jnp.where(fp_row == fp_last, jnp.exp(total_c - run_r), 0.0)
    rows[2] = jnp.where(fp_row < base, jnp.exp(run_r), 0.0)
    cbuf[3] = jnp.broadcast_to(jnp.where(fp_last < base, jnp.exp(total_c), 0.0), (heads, DIM))

    loaded("k", "v")
    pl.semaphore_wait(barrier, peers)
    kv_copies = {}
    for d in (4, 1, 3, 2):
        kv_copies[d] = push(
            kv.at[0], kv.at[d], kv_send.at[d - 1], kv_recv.at[d - 1], (seq_at(d), hd)
        )
        pl.when(exists(d))(kv_copies[d].start)
    c_copies = {}
    for d in (-3, -2, -1, 1, 2, 3):
        c_copies[d] = push(
            cbuf.at[3], cbuf.at[3 - d], c_send.at[d + 3], c_recv.at[3 - d], (seq_at(d), hd)
        )
        pl.when(exists(d))(c_copies[d].start)

        @pl.when(absent(d))
        def _(d=d):
            cbuf[3 + d] = jnp.zeros_like(cbuf[3 + d])

    for d in range(1, REACH + 1):

        @pl.when(absent(-d))
        def _(d=d):
            kv[d] = jnp.zeros_like(kv[d])

        @pl.when(absent(d))
        def _(d=d):
            dkv_in[d - 1] = jnp.zeros_like(dkv_in[d - 1])

    parity = lax.rem(me, 2)
    later = (parity == 1, parity == 0)
    sign = (1, -1)
    ahead = [jnp.where(later[w], sign[w], 3 * sign[w]) for w in (0, 1)]
    behind = [jnp.where(later[w], -3 * sign[w], -sign[w]) for w in (0, 1)]
    sends = [(None, exists(ahead[w]), exists(4 * sign[w])) for w in (0, 1)]
    gets = [(None, exists(behind[w]), exists(-4 * sign[w])) for w in (0, 1)]

    def when(condition, do):
        if condition is None:
            do()
        else:
            pl.when(condition)(do)

    for which in (0, 1):
        for stage in (1, 2):

            @pl.when(jnp.logical_not(gets[which][stage]))
            def _(which=which, stage=stage):
                st_in[which, stage] = jnp.zeros_like(st_in[which, stage])

    loaded("w", "r", "x", "g")
    wt[...] = flip(w_ref[...])
    rt[...] = flip(r_ref[...])

    each = heads // CHUNKS

    def state_copy(which, stage, c):
        step = (1 - 2 * parity, ahead[which], 4 * sign[which])[stage]
        source = (0, 1, jnp.where(later[which], 0, 1))[stage]
        part = pl.ds(c * each, each)
        return push(
            st_out.at[which, source, part],
            st_in.at[which, stage, part],
            st_send.at[which, stage, c],
            st_recv.at[which, stage, c],
            (lax.rem(me + step + n_seq, n_seq), hd),
        )

    def part_loop(c, _):
        for k in range(each):
            h = c * each + k
            scaled_w = (wt[...] * rows[1, pl.ds(h, 1), :]).astype(BF16)
            scaled_r = (rt[...] * rows[2, pl.ds(h, 1), :]).astype(BF16)
            st_out[0, 0, h] = nn(scaled_w, x_ref[:, cols(h)]).astype(BF16)
            st_out[1, 0, h] = nn(scaled_r, g_ref[:, cols(h)]).astype(BF16)
        for which in (0, 1):
            state_copy(which, 0, c).start()
            pl.when(later[which] & sends[which][2])(state_copy(which, 2, c).start)
        return 0

    lax.fori_loop(0, CHUNKS, part_loop, 0)

    tail_c = jnp.where(fp_col == fp_last, jnp.exp(total_r - run_c), 0.0)
    lead_c = jnp.where(fp_col < base, jnp.exp(run_c), 0.0)
    for h in range(heads):
        run_col[h] = run_c[:, h : h + 1]
        tail_col[h] = tail_c[:, h : h + 1]
        lead_col[h] = lead_c[:, h : h + 1]

    cross = nt(w_ref[...], r_ref[...])
    loaded("gain", "q", "og")
    head_lane = lax.broadcasted_iota(jnp.int32, (1, heads), 1)
    keep = (j0 <= j1) & (fp_col == fp_row)
    w_acc[...] = jnp.zeros_like(w_acc)

    def local_loop(h, _):
        x_h = x_ref[:, cols(h)]
        g_h = g_ref[:, cols(h)]
        corr = nt(x_h, g_h)
        dec = jnp.exp(jnp.where(keep, rows[0, pl.ds(h, 1), :] - run_col[h], NEG))
        w_acc[...] += corr * dec
        gain = jnp.sum(jnp.where(head_lane == h, gain_ref[...], 0.0), axis=1, keepdims=True)
        mix = (cross * dec).astype(BF16)
        gi_acc[:, cols(h)] = nn(mix, g_h) + gain * g_h.astype(F32)
        return 0

    lax.fori_loop(0, heads, local_loop, 0)
    for d, copy in c_copies.items():
        pl.when(exists(-d))(copy.wait_recv)
    for which in (0, 1):
        s = sign[which]
        c1, c2, c3 = [cbuf[3 - s * k] for k in (1, 2, 3)]
        own, partner = cbuf[3], cbuf[3 + s]
        one, zero = jnp.ones_like(own), jnp.zeros_like(own)
        coef[which, 0] = jnp.where(later[which], one, partner)
        coef[which, 1] = jnp.where(later[which], own, one)
        coef[which, 2] = jnp.where(later[which], one, zero)
        coef[which, 3] = jnp.where(later[which], c1, one)
        coef[which, 4] = jnp.where(later[which], c1 * c2 * c3, c1 * c2)

    def factor(which, i, h):
        return coef[which, i, pl.ds(h, 1), :]

    def pair_step(c, _=0):
        for which in (0, 1):
            state_copy(which, 0, c).wait_recv()
            for k in range(each):
                h = c * each + k
                st_out[which, 1, h] = (
                    factor(which, 0, h) * st_out[which, 0, h].astype(F32)
                    + factor(which, 1, h) * st_in[which, 0, h].astype(F32)
                ).astype(BF16)
            when(sends[which][1], state_copy(which, 1, c).start)
            pl.when(jnp.logical_not(later[which]) & sends[which][2])(state_copy(which, 2, c).start)
        return 0

    for i in range(q_heads):
        q_rows[i * tok : (i + 1) * tok] = q_ref[:, i * DIM : (i + 1) * DIM]
        og_rows[i * tok : (i + 1) * tok] = og_ref[:, i * DIM : (i + 1) * DIM]
    spot = lax.broadcasted_iota(jnp.int32, (tok, 1), 0).astype(F32)

    def head_lanes(i):
        return pl.ds(pl.multiple_of(i * tok, tok), tok)

    def score_step(o):
        kt[o] = flip(kv[o, 0]).astype(BF16)

        def one_head(i, _):
            key_pos = spot + (base - float(o * tok))
            allowed = key_pos >= fp_row
            if o == 0:
                allowed = allowed & (key_pos <= t_row)
            s_all[o, :, head_lanes(i)] = jnp.where(
                allowed, nt(kv[o, 0], q_ref[:, cols(i)]) * SCALE2, NEG
            )
            dp_all[o, :, head_lanes(i)] = nt(kv[o, 1], og_ref[:, cols(i)])
            return 0

        lax.fori_loop(0, q_heads, one_head, 0, unroll=True)

    def softmax_step(i):
        here = head_lanes(i)
        blocks = range(REACH + 1)
        scores = [s_all[o, :, here] for o in blocks]
        top = functools.reduce(jnp.maximum, [jnp.max(s, axis=0, keepdims=True) for s in scores])
        weights = [jnp.exp2(s - top) for s in scores]
        for o in blocks:
            s_all[o, :, here] = weights[o]
        norm = 1.0 / functools.reduce(
            jnp.add, [jnp.sum(e, axis=0, keepdims=True) for e in weights]
        )
        row_norm[:, here] = norm
        row_delta[:, here] = norm * functools.reduce(
            jnp.add,
            [jnp.sum(weights[o] * dp_all[o, :, here], axis=0, keepdims=True) for o in blocks],
        )

    def grad_step(d):
        def one_head(i, _):
            here = head_lanes(i)
            prob = s_all[d, :, here] * row_norm[:, here]
            ds = (prob * (dp_all[d, :, here] - row_delta[:, here])).astype(BF16)
            ds_all[d, :, here] = ds
            ph_all[d, :, here] = prob.astype(BF16)
            dq_acc[i] += nn(kt[d], ds)
            return 0

        lax.fori_loop(0, q_heads, one_head, 0, unroll=True)

    def kv_step(d):
        pl.when(exists(-d))(kv_copies[d].wait_recv)
        score_step(d)

    score_step(0)
    for d, c in zip((4, 1, 3, 2), range(CHUNKS)):
        pair_step(c)
        kv_step(d)

    def attend_loop(c, _):
        softmax_step(c)
        return 0

    dq_acc[...] = jnp.zeros_like(dq_acc)

    lax.fori_loop(0, CHUNKS, attend_loop, 0)

    def dkv_copy(d):
        return push(
            dkv_out.at[d - 1],
            dkv_in.at[d - 1],
            dkv_send.at[d - 1],
            dkv_recv.at[d - 1],
            (lax.rem(me - d + n_seq, n_seq), hd),
        )

    def grad_loop(step, _):
        d = step + 1
        grad_step(d)
        dkv_out[d - 1, 0] = (nn(ds_all[d], q_rows[...]) * SCALE).astype(BF16)
        dkv_out[d - 1, 1] = nn(ph_all[d], og_rows[...]).astype(BF16)
        pl.when(me >= d)(dkv_copy(d).start)
        return 0

    lax.fori_loop(0, REACH, grad_loop, 0)
    grad_step(0)
    for i in range(q_heads):
        gq_ref[:, i * DIM : (i + 1) * DIM] = (jnp.transpose(dq_acc[i]) * SCALE).astype(BF16)
    own_grad[0] = nn(ds_all[0], q_rows[...]) * SCALE
    own_grad[1] = nn(ph_all[0], og_rows[...])
    w_sum = w_acc[...]
    gw = nn(w_sum.astype(BF16), r_ref[...])
    gr = nn(flip(w_sum).astype(BF16), w_ref[...])
    for c in range(n_head):
        tot[c, 0] = gw[c * (tok // n_head) : (c + 1) * (tok // n_head)]
        tot[c, 1] = gr[c * (tok // n_head) : (c + 1) * (tok // n_head)]

    def arrived(which, h):
        return (
            factor(which, 2, h) * st_in[which, 0, h].astype(F32)
            + factor(which, 3, h) * st_in[which, 1, h].astype(F32)
            + factor(which, 4, h) * st_in[which, 2, h].astype(F32)
        ).astype(BF16)

    def carry_loop(c, sums):
        gw, gr = sums
        for which in (0, 1):
            for stage in (1, 2):
                pl.when(gets[which][stage])(state_copy(which, stage, c).wait_recv)
        for k in range(each):
            h = c * each + k
            state, adjoint = arrived(0, h), arrived(1, h)
            x_h = x_ref[:, cols(h)]
            g_h = g_ref[:, cols(h)]
            tail_h, lead_h = tail_col[h], lead_col[h]
            gi_ref[:, cols(h)] = (
                gi_acc[:, cols(h)] + nn(w_ref[...], adjoint) * tail_h
            ).astype(BF16)
            gw += nt(x_h, adjoint) * tail_h
            gr += nt(g_h, state) * lead_h
        return gw, gr

    zeros = jnp.zeros((tok, DIM), F32)
    gw, gr = lax.fori_loop(0, CHUNKS, carry_loop, (zeros, zeros))
    rows_each = tok // n_head
    for c in range(n_head):
        for i, total in enumerate((gw, gr)):
            part = tot[c, i] + total[c * rows_each : (c + 1) * rows_each]
            tot[c, i] = part
            rs_out[c, i] = part.astype(BF16)
    rs_copies = []
    for p in range(1, n_head):
        to = head_at(p)
        copy = push(rs_out.at[to], rs_in.at[p - 1], rs_send.at[p - 1], rs_recv.at[p - 1], (me, to))
        copy.start()
        rs_copies.append(copy)

    gk, gv = own_grad[0], own_grad[1]
    for d in (4, 3, 2, 1):
        pl.when(exists(d))(dkv_copy(d).wait_recv)
        gk += dkv_in[d - 1, 0].astype(F32)
        gv += dkv_in[d - 1, 1].astype(F32)
    gk_ref[...] = gk.astype(BF16)
    gv_ref[...] = gv.astype(BF16)

    gw_out = tot[hd, 0]
    gr_out = tot[hd, 1]
    for p in range(1, n_head):
        rs_copies[p - 1].wait_recv()
        gw_out += rs_in[p - 1, 0].astype(F32)
        gr_out += rs_in[p - 1, 1].astype(F32)
    gw_ref[...] = gw_out
    gr_ref[...] = gr_out

    for d, copy in kv_copies.items():
        pl.when(exists(d))(copy.wait_send)
    for d, copy in c_copies.items():
        pl.when(exists(d))(copy.wait_send)

    def drain(c, _):
        for which in (0, 1):
            for stage in range(3):
                when(sends[which][stage], state_copy(which, stage, c).wait_send)
        pl.when(me > c)(dkv_copy(c + 1).wait_send)
        return 0

    lax.fori_loop(0, CHUNKS, drain, 0)

    for copy in rs_copies:
        copy.wait_send()


def store(*refs):
    *refs, sem = refs
    count = len(refs) // 2
    copies = [
        pltpu.make_async_copy(refs[i], refs[count + i], sem.at[i]) for i in range(count)
    ]
    for copy in copies:
        copy.start()
    for copy in copies:
        copy.wait()


def on_device(n_seq, n_head, *args):
    (x, g, w, r, step, rate, gain, q, k, v, og, docs) = args
    tok, heads = x.shape[0], step.shape[0]
    vmem = pl.BlockSpec(memory_space=pltpu.VMEM)
    hbm = pl.BlockSpec(memory_space=pltpu.HBM)
    rows_each = tok // n_head
    dma = pltpu.SemaphoreType.DMA
    scratch = [
        pltpu.VMEM(x.shape, BF16),
        pltpu.VMEM(g.shape, BF16),
        pltpu.VMEM(w.shape, BF16),
        pltpu.VMEM(r.shape, BF16),
        pltpu.VMEM(step.shape, F32),
        pltpu.VMEM((1, heads), F32),
        pltpu.VMEM((1, heads), F32),
        pltpu.VMEM(q.shape, BF16),
        pltpu.VMEM(og.shape, BF16),
        pltpu.VMEM((1, docs.shape[0]), jnp.int32),
        pltpu.VMEM((REACH + 1, 2, tok, DIM), BF16),
        pltpu.VMEM((REACH + 1, DIM, tok), BF16),
        pltpu.VMEM((q.shape[1] // DIM * tok, DIM), BF16),
        pltpu.VMEM((q.shape[1] // DIM * tok, DIM), BF16),
        pltpu.VMEM((REACH + 1, tok, q.shape[1] // DIM * tok), F32),
        pltpu.VMEM((REACH + 1, tok, q.shape[1] // DIM * tok), F32),
        pltpu.VMEM((1, q.shape[1] // DIM * tok), F32),
        pltpu.VMEM((1, q.shape[1] // DIM * tok), F32),
        pltpu.VMEM((q.shape[1] // DIM, DIM, tok), F32),
        pltpu.VMEM((REACH + 1, tok, q.shape[1] // DIM * tok), BF16),
        pltpu.VMEM((REACH + 1, tok, q.shape[1] // DIM * tok), BF16),
        pltpu.VMEM((2, tok, DIM), F32),
        pltpu.VMEM((REACH, 2, tok, DIM), BF16),
        pltpu.VMEM((REACH, 2, tok, DIM), BF16),
        pltpu.VMEM((7, heads, DIM), F32),
        pltpu.VMEM((2, 2, heads, DIM, DIM), BF16),
        pltpu.VMEM((2, 3, heads, DIM, DIM), BF16),
        pltpu.VMEM((DIM, tok), F32),
        pltpu.VMEM((DIM, tok), F32),
        pltpu.VMEM((3, heads, tok), F32),
        pltpu.VMEM((heads, tok, 1), F32),
        pltpu.VMEM((heads, tok, 1), F32),
        pltpu.VMEM((heads, tok, 1), F32),
        pltpu.VMEM((tok, heads * DIM), F32),
        pltpu.VMEM((tok, tok), F32),
        pltpu.VMEM((2, 5, heads, DIM), F32),
        pltpu.VMEM((n_head, 2, rows_each, DIM), F32),
        pltpu.VMEM((n_head, 2, rows_each, DIM), BF16),
        pltpu.VMEM((n_head - 1, 2, rows_each, DIM), BF16),
        dma((len(args),)),
        dma((REACH,)),
        dma((REACH,)),
        dma((7,)),
        dma((7,)),
        dma((2, 3, CHUNKS)),
        dma((2, 3, CHUNKS)),
        dma((REACH,)),
        dma((REACH,)),
        dma((n_head - 1,)),
        dma((n_head - 1,)),
    ]
    made = pl.pallas_call(
        functools.partial(kernel, n_seq, n_head),
        out_shape=(
            jax.ShapeDtypeStruct(x.shape, BF16),
            jax.ShapeDtypeStruct((rows_each, DIM), F32),
            jax.ShapeDtypeStruct((rows_each, DIM), F32),
            jax.ShapeDtypeStruct(q.shape, BF16),
            jax.ShapeDtypeStruct(k.shape, BF16),
            jax.ShapeDtypeStruct(v.shape, BF16),
        ),
        in_specs=[hbm] * len(args),
        out_specs=(vmem,) * 6,
        scratch_shapes=scratch,
        compiler_params=pltpu.CompilerParams(
            collective_id=0, has_side_effects=True, vmem_limit_bytes=48 * 2**20
        ),
    )(*[pltpu.with_memory_space_constraint(a, pltpu.HBM) for a in (x, g, w, r, step, rate.reshape(1, -1), gain.reshape(1, -1), q, k, v, og, docs.reshape(1, -1))])
    return pl.pallas_call(
        store,
        out_shape=[jax.ShapeDtypeStruct(m.shape, m.dtype) for m in made],
        in_specs=[vmem] * len(made),
        out_specs=[hbm] * len(made),
        scratch_shapes=[dma((len(made),))],
        compiler_params=pltpu.CompilerParams(vmem_limit_bytes=2 * 2**20),
    )(*made)


def solution(mesh):
    placed = (
        P("seq", "head"),
        P("seq", "head"),
        P("seq", None),
        P("seq", None),
        P("head", "seq"),
        P("head"),
        P("head"),
        P("seq", "head"),
        P("seq", "head"),
        P("seq", "head"),
        P("seq", "head"),
        P(),
    )
    return jax.shard_map(
        functools.partial(on_device, mesh.shape["seq"], mesh.shape["head"]),
        mesh=mesh,
        in_specs=placed,
        out_specs=(
            P("seq", "head"),
            P(("seq", "head"), None),
            P(("seq", "head"), None),
            P("seq", "head"),
            P("seq", "head"),
            P("seq", "head"),
        ),
        check_vma=False,
    )
```
